32 devices in a mesh: lat: 4 (over y, x), ma: 8 (over z, core).
Axes of the slice: x: 2, y: 2, z: 4, core: 2. Of those that a mesh axis runs over, the one named last changes fastest.
Arguments:
- fourier: bfloat16 [16, 2, 256, 2560], P(None, None, 'ma', 'lat'), may hold values from -6 to 6
- legendre: bfloat16 [16, 1280, 2, 640], P('ma', 'lat'), may hold values from -0.125 to 0.125
- window: int32 [16], replicated, may hold values from 0 to 639, as said below
- assign: int32 [16], replicated, may hold values from 0 to 15, each once
Outputs:
- coefficients: float32 [16, 2, 640, 256], P('ma', None, 'lat')
The draws below stay inside these ranges and needn't reach their ends.
Inputs may be any that keep to these rules, and one draw needn't show every extreme that they name: `window`: distinct group numbers; 0 and 639 are always among them. `assign`: every position from 0 to 15 appears once.
All inputs are finite; a program needn't handle non-finite values.
Results may differ from the reference program's by a relative error of at most 0.017.
Values may be sent and summed in bfloat16 or wider, within the bound.
A program may use at most 64 MiB of HBM per device.

```python
import jax
import jax.numpy as jnp
from jax import lax

NLAT = 2560
NWAVE = 1280
FIELDS = 256
GROUPS = 16
LATH = 1280
KCOLS = 640
N_LAT = 4


def draw_window(key, part):
    group_count = NWAVE // 2
    inner = jax.random.permutation(key, group_count - 2).astype(jnp.int32) + 1
    ends = jnp.array([0, group_count - 1], dtype=jnp.int32)
    chosen = jnp.concatenate([ends, inner[:GROUPS - 2]])
    shuffle = jax.random.permutation(jax.random.fold_in(key, 7), GROUPS)
    return chosen[shuffle].astype(jnp.int32)


def steps_of(key, dims, split, smallest, top_value):
    gain = 1.0
    for axis_at, parts in split:
        heights = jax.random.uniform(jax.random.fold_in(jax.random.fold_in(key, 6), axis_at), (parts,), jnp.float32, smallest / len(split), top_value / len(split))
        gain = gain * jnp.repeat(jnp.exp(heights), dims[axis_at] // parts).reshape((-1,) + (1,) * (len(dims) - 1 - axis_at))
    return gain


def scatter_about(rng, extent, spread, bound, split=(), kind=jnp.bfloat16):
    result = jax.random.normal(rng, extent, jnp.float32) * spread
    if len(split) > 0:
        result = steps_of(rng, extent, split, -0.22, 0.18) * result
    return jnp.clip(result, min=-bound, max=bound).astype(kind)


def setup_inputs(seed: int = 0) -> dict:
    key_list = jax.random.split(jax.random.key(seed), 5)
    return {
        "fourier": scatter_about(key_list[0], (GROUPS, 2, FIELDS, NLAT), 1.0, 6.0, ((2, 8), (3, 4))),
        "legendre": scatter_about(key_list[1], (GROUPS, LATH, 2, KCOLS), NLAT ** -0.5, 0.125, ((0, 8), (1, 4))),
        "window": draw_window(jax.random.fold_in(key_list[4], 71), 0),
        "assign": jax.random.permutation(key_list[3], GROUPS).astype(jnp.int32),
    }


def pair_source():
    pair_dev = NLAT // (2 * N_LAT)
    hemi_dev = N_LAT // 2
    blocks = jnp.arange(N_LAT, dtype=jnp.int32)
    within = jnp.arange(pair_dev, dtype=jnp.int32)
    starts = 2 * pair_dev * (blocks % hemi_dev) + pair_dev * (blocks // hemi_dev)
    return (starts[:, None] + within[None, :]).reshape(-1).astype(jnp.int32)


def reference(fourier, legendre, window, assign):
    pair_dev = NLAT // (2 * N_LAT)
    half_lat = NLAT // 2
    column_count = NWAVE // 2
    source_rows = pair_source()
    column_base = 2 * jnp.arange(column_count, dtype=jnp.int32)

    def one_group(position):
        slot_index = assign[position]
        stored = lax.dynamic_index_in_dim(fourier, slot_index, 0, keepdims=False)
        latitudes = jnp.transpose(stored, (2, 0, 1)).astype(jnp.float32)
        northern = latitudes[:half_lat]
        southern = latitudes[half_lat:]
        sym_part = (northern + southern).astype(jnp.bfloat16)[source_rows]
        anti_part = (northern - southern).astype(jnp.bfloat16)[source_rows]
        group_id = window[slot_index]
        table_part = lax.dynamic_index_in_dim(legendre, position, 0, keepdims=False)
        results = []
        for parity in range(2):
            column = column_base + parity
            upper_slot = (column >= NWAVE - group_id)[None, :]
            weights = table_part[:, parity, :].astype(jnp.float32)
            lower_table = jnp.where(upper_slot, 0.0, weights).reshape(N_LAT, pair_dev, column_count)
            upper_table = jnp.where(upper_slot, weights, 0.0).reshape(N_LAT, pair_dev, column_count)
            leading = (sym_part if parity == 0 else anti_part)[:, 0, :]
            leading = leading.astype(jnp.float32).reshape(N_LAT, pair_dev, FIELDS)
            trailing = jnp.where((parity + group_id) % 2 == 1, anti_part[:, 1, :], sym_part[:, 1, :])
            trailing = trailing.astype(jnp.float32).reshape(N_LAT, pair_dev, FIELDS)
            partial_value = jnp.einsum("dpk,dpf->dkf", lower_table, leading, precision=lax.Precision.HIGHEST)
            partial_value = partial_value + jnp.einsum("dpk,dpf->dkf", upper_table, trailing, precision=lax.Precision.HIGHEST)
            rounded = lax.optimization_barrier(partial_value.astype(jnp.bfloat16))
            results.append(jnp.sum(rounded.astype(jnp.float32), axis=0))
        return jnp.stack(results, axis=0)

    return lax.map(one_group, jnp.arange(GROUPS, dtype=jnp.int32))
```

```python
import functools

import jax
import jax.numpy as jnp
from jax import lax
from jax.experimental import pallas as pl
from jax.experimental.pallas import tpu as pltpu
from jax.sharding import PartitionSpec as P

MESH = pl.DeviceIdType.MESH
BF16 = jnp.bfloat16
F32 = jnp.float32


def swapped(value, axis, bit):
    mask = 2**bit
    pairs = [(source, source ^ mask) for source in range(lax.axis_size(axis))]
    return lax.ppermute(value, axis, pairs)


def fold_pairs(latitudes, northern):
    pair_rows = latitudes.shape[3] // 2
    leading_rows = latitudes[:, :, :, :pair_rows]
    trailing_rows = latitudes[:, :, :, pair_rows:]
    outgoing = jnp.where(northern, trailing_rows, leading_rows)
    bit_number = lax.axis_size("lat").bit_length() - 2
    arrived = swapped(outgoing, "lat", bit_number)
    staying = jnp.where(northern, leading_rows, trailing_rows)
    upper_rows = jnp.where(northern, staying, arrived).astype(F32)
    lower_rows = jnp.where(northern, arrived, staying).astype(F32)
    return (
        (upper_rows + lower_rows).astype(BF16),
        (upper_rows - lower_rows).astype(BF16),
    )


def plain_on_device(fourier, legendre, window, assign):
    local_groups = legendre.shape[0]
    lat_count = lax.axis_size("lat")
    northern = lax.axis_index("lat") < lat_count // 2
    count = assign.shape[0]
    chosen = assign[:, None] == lax.iota(jnp.int32, count)[None, :]
    ordered = jnp.einsum(
        "iw,wsfr->isfr", chosen.astype(BF16), fourier, preferred_element_type=F32
    ).astype(BF16)
    gathered = lax.all_to_all(ordered, "ma", split_axis=0, concat_axis=2, tiled=True)
    sym_part, anti_part = fold_pairs(gathered, northern)
    all_ids = jnp.sum(jnp.where(chosen, window[None, :], 0), axis=1)
    group_ids = lax.dynamic_slice_in_dim(
        all_ids, lax.axis_index("ma") * local_groups, local_groups
    )
    column_count = legendre.shape[3]
    wave_total = 2 * column_count
    zero_value = jnp.zeros((), BF16)

    def half_term(parity):
        column = 2 * lax.iota(jnp.int32, column_count) + parity
        upper_slot = (column[None, :] >= wave_total - group_ids[:, None])[:, None, :]
        table_part = legendre[:, :, parity, :]
        masked = jnp.stack(
            [
                jnp.where(upper_slot, zero_value, table_part),
                jnp.where(upper_slot, table_part, zero_value),
            ],
            axis=1,
        )
        leading = sym_part[:, 0] if parity == 0 else anti_part[:, 0]
        flipped = ((group_ids + parity) % 2 == 1)[:, None, None]
        trailing = jnp.where(flipped, anti_part[:, 1], sym_part[:, 1])
        sources = jnp.stack([leading, trailing], axis=1)
        return jnp.einsum("gspk,gsfp->gkf", masked, sources, preferred_element_type=F32)

    partials = jnp.stack([half_term(0), half_term(1)], axis=1)
    return lax.psum_scatter(
        partials.astype(BF16), "lat", scatter_dimension=2, tiled=True
    ).astype(F32)


def fused_kernel(
    lat_n,
    ma_n,
    assign_ref,
    window_ref,
    four_hbm,
    leg_hbm,
    out_hbm,
    out_ref,
    four_ref,
    leg_ref,
    stage,
    recv,
    weight,
    part,
    landed,
    send_sem,
    recv_sem,
    psend_sem,
    precv_sem,
    leg_sem,
    four_sem,
    out_sem,
    here_sem,
):
    groups_here = leg_ref.shape[0]
    fields_here = four_ref.shape[2]
    rows = four_ref.shape[3]
    pair = rows // 2
    body = pair // 128 * 128
    tail = pair - body
    kcols = leg_ref.shape[3]
    block = kcols // lat_n
    hemi = lat_n // 2
    half_ma = ma_n // 2
    half_f = half_ma * fields_here

    lat = lax.axis_index("lat")
    ma = lax.axis_index("ma")
    side = lat // hemi
    mine = side
    partner = lax.rem(lat + hemi, lat_n)
    my_half = ma // half_ma

    rows_copy = pltpu.make_async_copy(four_hbm, four_ref, four_sem)
    rows_copy.start()
    table_copy = pltpu.make_async_copy(leg_hbm, leg_ref, leg_sem)
    table_copy.start()

    far = lax.rem(ma + half_ma, ma_n)
    far_first = (1 - my_half) * half_ma
    near_first = my_half * half_ma
    low = lax.rem(ma, 2)

    barrier = pltpu.get_barrier_semaphore()
    met = 0
    for m in range(half_ma):
        for there in (lat, partner):
            pl.semaphore_signal(
                barrier, inc=1, device_id=(there, far_first + m), device_id_type=MESH
            )
            met += 1
    for r in range(1, lat_n):
        if r != hemi:
            pl.semaphore_signal(
                barrier, inc=1, device_id=(lax.rem(lat + r, lat_n), far), device_id_type=MESH
            )
            met += 1

    def pack(q, g):
        slab = four_ref.at[assign_ref[q * groups_here + g]]
        for t in range(2):
            at, rest = t * (pair + tail), body + t * tail
            stage[g, q, t] = jnp.concatenate(
                [slab[n, :, at : at + body] for n in range(2)]
                + [slab[n, :, rest : rest + tail] for n in range(2)],
                axis=1,
            )

    def row_copy(g, q, own):
        t = mine if own else 1 - mine
        return pltpu.make_async_remote_copy(
            src_ref=stage.at[g, q, t],
            dst_ref=recv.at[g, side, ma],
            send_sem=send_sem.at[g, q, t],
            recv_sem=recv_sem.at[g, side, ma],
            device_id=(lat if own else partner, q),
            device_id_type=MESH,
        )

    def place(hop):
        return hop // 2 * 2 + lax.rem(hop + low, 2)

    def send_far(hop, g):
        q = far_first + place(hop)
        pack(q, g)
        row_copy(g, q, False).start()
        row_copy(g, q, True).start()

    def send_near(hop, g):
        q = near_first + place(hop)
        pack(q, g)
        row_copy(g, q, False).start()

        @pl.when(q != ma)
        def _():
            row_copy(g, q, True).start()

        @pl.when(q == ma)
        def _():
            pltpu.make_async_copy(
                stage.at[g, q, mine], recv.at[g, side, ma], recv_sem.at[g, side, ma]
            ).start()

    def each_hop(step):
        def body_of(hop, c):
            step(hop)
            return c

        lax.fori_loop(0, half_ma, body_of, 0)

    rows_copy.wait()
    pl.semaphore_wait(barrier, met)
    pl.semaphore_signal(here_sem, inc=1, device_id=(lat, far), device_id_type=MESH)
    each_hop(lambda hop: send_far(hop, 0))
    pl.semaphore_wait(here_sem, 1)
    each_hop(lambda hop: send_near(hop, 0))

    def both(hop):
        send_far(hop, 1)
        send_near(hop, 1)

    each_hop(both)
    table_copy.wait()

    ids = [window_ref[assign_ref[ma * groups_here + g]] for g in range(groups_here)]
    for g in range(groups_here):
        for e in range(2):

            def fill(j, c, g=g, e=e):
                start = pl.multiple_of(j * 128, 128)
                table = jnp.concatenate(
                    [
                        leg_ref[g, pl.ds(mine * tail, body), e, pl.ds(start, 128)],
                        leg_ref[g, pl.ds((1 - mine) * body, tail), e, pl.ds(start, 128)],
                    ],
                    axis=0,
                ).astype(F32).T
                k = start + lax.broadcasted_iota(jnp.int32, (128, 1), 0)
                under = 2 * k + e < 2 * kcols - ids[g]
                lower = jnp.where(under, table, 0.0)
                upper = jnp.where(under, 0.0, table)
                weight[g, e, pl.ds(start, 128), :] = jnp.concatenate(
                    [lower[:, :body], upper[:, :body], lower[:, body:], upper[:, body:]],
                    axis=1,
                ).astype(BF16)
                return c

            lax.fori_loop(0, kcols // 128, fill, 0)

    lane = lax.broadcasted_iota(jnp.int32, (1, rows), 1)
    in_upper = ((lane >= body) & (lane < 2 * body)) | (lane >= 2 * body + tail)

    def part_copy(g, h, e, r):
        there = lax.rem(lat + r, lat_n)
        return pltpu.make_async_remote_copy(
            src_ref=part.at[g, h, there, e],
            dst_ref=landed.at[r - 1, g, h, e],
            send_sem=psend_sem.at[r - 1, g, h, e],
            recv_sem=precv_sem.at[r - 1, g, h, e],
            device_id=(there, ma),
            device_id_type=MESH,
        )

    def multiply(g, h):
        def arrive(m, c):
            for ns in range(2):
                piece = recv.at[g, ns, h * half_ma + m]
                pltpu.make_async_copy(piece, piece, recv_sem.at[g, ns, h * half_ma + m]).wait()
            return c

        lax.fori_loop(0, half_ma, arrive, 0)
        north = recv[g, 0, pl.ds(h * half_ma, half_ma)].reshape(half_f, rows).astype(F32)
        south = recv[g, 1, pl.ds(h * half_ma, half_ma)].reshape(half_f, rows).astype(F32)
        for e in range(2):
            odd = lax.rem(ids[g] + e, 2).astype(F32)
            sign = jnp.where(in_upper, 1.0 - 2.0 * odd, 1.0 - 2.0 * e)
            source = (north + sign * south).astype(BF16)
            for r in (*range(1, lat_n), 0):
                d = lax.rem(lat + r, lat_n)
                part[g, h, d, e] = lax.dot_general(
                    weight[g, e, pl.ds(pl.multiple_of(d * block, 16), block), :],
                    source,
                    (((1,), (1,)), ((), ())),
                    preferred_element_type=F32,
                ).astype(BF16)
                if r:
                    part_copy(g, h, e, r).start()

    def out_copy(g, h, e):
        at = pl.multiple_of(h * half_f, 128)
        return pltpu.make_async_copy(
            out_ref.at[g, e, h], out_hbm.at[g, e, :, pl.ds(at, half_f)], out_sem.at[g, e, h]
        )

    def finish(g, h):
        for e in range(2):
            for r in range(1, lat_n):
                part_copy(g, h, e, r).wait_recv()
            total = part[g, h, lat, e].astype(F32)
            for r in range(1, lat_n):
                total = total + landed[r - 1, g, h, e].astype(F32)
            out_ref[g, e, h] = total
            out_copy(g, h, e).start()

    chunks = [(g, (my_half + j) % 2) for g in range(groups_here) for j in range(2)]
    for i, (g, h) in enumerate(chunks):
        multiply(g, h)
        if i:
            finish(*chunks[i - 1])
    finish(*chunks[-1])

    for g in range(groups_here):

        def sent(q, c, g=g):
            row_copy(g, q, False).wait_send()

            @pl.when(q != ma)
            def _():
                row_copy(g, q, True).wait_send()

            return c

        lax.fori_loop(0, ma_n, sent, 0)
    for g, h in chunks:
        for e in range(2):
            for r in range(1, lat_n):
                part_copy(g, h, e, r).wait_send()
            out_copy(g, h, e).wait()


def fused_on_device(fourier, legendre, window, assign):
    lat_n, ma_n = lax.axis_size("lat"), lax.axis_size("ma")
    _, slots, fields_here, rows = fourier.shape
    groups_here, pair, parities, kcols = legendre.shape
    block = kcols // lat_n
    fields = fields_here * ma_n
    smem = pl.BlockSpec(memory_space=pltpu.SMEM)
    hbm = pl.BlockSpec(memory_space=pltpu.HBM)
    dma = pltpu.SemaphoreType.DMA
    return pl.pallas_call(
        functools.partial(fused_kernel, lat_n, ma_n),
        out_shape=jax.ShapeDtypeStruct((groups_here, 2, block, fields), F32),
        in_specs=[smem, smem, hbm, hbm],
        out_specs=hbm,
        scratch_shapes=[
            pltpu.VMEM((groups_here, 2, 2, block, fields // 2), F32),
            pltpu.VMEM(fourier.shape, BF16),
            pltpu.VMEM(legendre.shape, BF16),
            pltpu.VMEM((groups_here, ma_n, 2, fields_here, rows), BF16),
            pltpu.VMEM((groups_here, 2, ma_n, fields_here, rows), BF16),
            pltpu.VMEM((groups_here, 2, kcols, rows), BF16),
            pltpu.VMEM((groups_here, 2, lat_n, 2, block, fields // 2), BF16),
            pltpu.VMEM((lat_n - 1, groups_here, 2, 2, block, fields // 2), BF16),
            dma((groups_here, ma_n, 2)),
            dma((groups_here, 2, ma_n)),
            dma((lat_n - 1, groups_here, 2, 2)),
            dma((lat_n - 1, groups_here, 2, 2)),
            dma,
            dma,
            dma((groups_here, 2, 2)),
            pltpu.SemaphoreType.REGULAR,
        ],
        compiler_params=pltpu.CompilerParams(
            collective_id=0, has_side_effects=True, vmem_limit_bytes=63 * 2**20
        ),
        cost_estimate=pl.CostEstimate(
            flops=8 * groups_here * kcols * rows * fields,
            bytes_accessed=2 * (fourier.size + legendre.size),
            transcendentals=0,
        ),
    )(assign, window, fourier, legendre)


def fits_kernel(mesh, fourier, legendre):
    lat_n, ma_n = mesh.shape["lat"], mesh.shape["ma"]
    fields_here = fourier.shape[2] // ma_n
    pair = legendre.shape[1] // lat_n
    block = legendre.shape[3] // lat_n
    return (
        fourier.shape[1] == 2
        and lat_n == 4
        and ma_n == 8
        and legendre.shape[0] == 2 * ma_n
        and fields_here % 16 == 0
        and (fields_here * ma_n) % 256 == 0
        and (2 * pair) % 128 == 0
        and block % 16 == 0
        and legendre.shape[3] % 128 == 0
    )


def solution(mesh):
    def run(fourier, legendre, window, assign):
        fused = fits_kernel(mesh, fourier, legendre)
        return jax.shard_map(
            fused_on_device if fused else plain_on_device,
            mesh=mesh,
            in_specs=(P(None, None, "ma", "lat"), P("ma", "lat", None, None), P(), P()),
            out_specs=P("ma", None, "lat", None),
            check_vma=False,
        )(fourier, legendre, window, assign)

    return run
```

```python
import functools

import jax
import jax.numpy as jnp
from jax import lax
from jax.experimental import pallas as pl
from jax.experimental.pallas import tpu as pltpu
from jax.sharding import PartitionSpec as P

MESH = pl.DeviceIdType.MESH
BF16 = jnp.bfloat16
F32 = jnp.float32


def swapped(value, axis, bit):
    mask = 2**bit
    pairs = [(source, source ^ mask) for source in range(lax.axis_size(axis))]
    return lax.ppermute(value, axis, pairs)


def fold_pairs(latitudes, northern):
    pair_rows = latitudes.shape[3] // 2
    leading_rows = latitudes[:, :, :, :pair_rows]
    trailing_rows = latitudes[:, :, :, pair_rows:]
    outgoing = jnp.where(northern, trailing_rows, leading_rows)
    bit_number = lax.axis_size("lat").bit_length() - 2
    arrived = swapped(outgoing, "lat", bit_number)
    staying = jnp.where(northern, leading_rows, trailing_rows)
    upper_rows = jnp.where(northern, staying, arrived).astype(F32)
    lower_rows = jnp.where(northern, arrived, staying).astype(F32)
    return (
        (upper_rows + lower_rows).astype(BF16),
        (upper_rows - lower_rows).astype(BF16),
    )


def plain_on_device(fourier, legendre, window, assign):
    local_groups = legendre.shape[0]
    lat_count = lax.axis_size("lat")
    northern = lax.axis_index("lat") < lat_count // 2
    count = assign.shape[0]
    chosen = assign[:, None] == lax.iota(jnp.int32, count)[None, :]
    ordered = jnp.einsum(
        "iw,wsfr->isfr", chosen.astype(BF16), fourier, preferred_element_type=F32
    ).astype(BF16)
    gathered = lax.all_to_all(ordered, "ma", split_axis=0, concat_axis=2, tiled=True)
    sym_part, anti_part = fold_pairs(gathered, northern)
    all_ids = jnp.sum(jnp.where(chosen, window[None, :], 0), axis=1)
    group_ids = lax.dynamic_slice_in_dim(
        all_ids, lax.axis_index("ma") * local_groups, local_groups
    )
    column_count = legendre.shape[3]
    wave_total = 2 * column_count
    zero_value = jnp.zeros((), BF16)

    def half_term(parity):
        column = 2 * lax.iota(jnp.int32, column_count) + parity
        upper_slot = (column[None, :] >= wave_total - group_ids[:, None])[:, None, :]
        table_part = legendre[:, :, parity, :]
        masked = jnp.stack(
            [
                jnp.where(upper_slot, zero_value, table_part),
                jnp.where(upper_slot, table_part, zero_value),
            ],
            axis=1,
        )
        leading = sym_part[:, 0] if parity == 0 else anti_part[:, 0]
        flipped = ((group_ids + parity) % 2 == 1)[:, None, None]
        trailing = jnp.where(flipped, anti_part[:, 1], sym_part[:, 1])
        sources = jnp.stack([leading, trailing], axis=1)
        return jnp.einsum("gspk,gsfp->gkf", masked, sources, preferred_element_type=F32)

    partials = jnp.stack([half_term(0), half_term(1)], axis=1)
    return lax.psum_scatter(
        partials.astype(BF16), "lat", scatter_dimension=2, tiled=True
    ).astype(F32)


def fused_kernel(
    lat_n,
    ma_n,
    assign_hbm,
    window_hbm,
    four_hbm,
    leg_hbm,
    out_ref,
    assign_ref,
    window_ref,
    four_ref,
    leg_ref,
    stage,
    recv,
    weight,
    part,
    relay,
    send_sem,
    recv_sem,
    psend_sem,
    precv_sem,
    own_sem,
    load_sem,
    here_sem,
):
    groups_here = leg_ref.shape[0]
    fields_here = four_ref.shape[2]
    rows = four_ref.shape[3]
    pair = rows // 2
    body = pair // 128 * 128
    tail = pair - body
    kcols = leg_ref.shape[3]
    block = kcols // lat_n
    hemi = lat_n // 2
    half_ma = ma_n // 2
    half_f = half_ma * fields_here

    lat = lax.axis_index("lat")
    ma = lax.axis_index("ma")
    side = lat // hemi
    mine = side
    partner = lax.rem(lat + hemi, lat_n)
    my_half = ma // half_ma

    beside = lat + 1 - 2 * lax.rem(lat, 2)
    across = lax.rem(beside + hemi, lat_n)

    assign_copy = pltpu.make_async_copy(assign_hbm, assign_ref, load_sem.at[0])
    window_copy = pltpu.make_async_copy(window_hbm, window_ref, load_sem.at[1])
    rows_copy = pltpu.make_async_copy(four_hbm, four_ref, load_sem.at[2])
    table_copy = pltpu.make_async_copy(leg_hbm, leg_ref, load_sem.at[3])
    assign_copy.start()
    rows_copy.start()

    far = lax.rem(ma + half_ma, ma_n)
    far_first = (1 - my_half) * half_ma
    near_first = my_half * half_ma
    low = lax.rem(ma, 2)

    barrier = pltpu.get_barrier_semaphore()
    met = 0
    for m in range(half_ma):
        for there in (lat, partner):
            pl.semaphore_signal(
                barrier, inc=1, device_id=(there, far_first + m), device_id_type=MESH
            )
            met += 1
    for there in (beside, across):
        pl.semaphore_signal(barrier, inc=1, device_id=(there, far), device_id_type=MESH)
        met += 1
    window_copy.start()
    table_copy.start()

    def pack(q, g):
        slab = four_ref.at[assign_ref[q * groups_here + g]]
        for t in range(2):
            at, rest = t * (pair + tail), body + t * tail
            stage[g, q, t] = jnp.concatenate(
                [slab[n, :, at : at + body] for n in range(2)]
                + [slab[n, :, rest : rest + tail] for n in range(2)],
                axis=1,
            )

    def row_copy(g, q, own):
        t = mine if own else 1 - mine
        return pltpu.make_async_remote_copy(
            src_ref=stage.at[g, q, t],
            dst_ref=recv.at[g, side, ma],
            send_sem=send_sem.at[g, q, t],
            recv_sem=recv_sem.at[g, side, ma],
            device_id=(lat if own else partner, q),
            device_id_type=MESH,
        )

    def place(hop):
        return hop // 2 * 2 + lax.rem(hop + low, 2)

    def send_far(hop, g):
        q = far_first + place(hop)
        pack(q, g)
        row_copy(g, q, False).start()
        row_copy(g, q, True).start()

    def send_near(hop, g):
        q = near_first + place(hop)
        pack(q, g)
        row_copy(g, q, False).start()

        @pl.when(q != ma)
        def _():
            row_copy(g, q, True).start()

        @pl.when(q == ma)
        def _():
            pltpu.make_async_copy(
                stage.at[g, q, mine], recv.at[g, side, ma], recv_sem.at[g, side, ma]
            ).start()

    def each_hop(step):
        def body_of(hop, c):
            step(hop)
            return c

        lax.fori_loop(0, half_ma, body_of, 0)

    assign_copy.wait()
    rows_copy.wait()
    pl.semaphore_wait(barrier, met)
    pl.semaphore_signal(here_sem, inc=1, device_id=(lat, far), device_id_type=MESH)
    each_hop(lambda hop: send_far(hop, 0))
    pl.semaphore_wait(here_sem, 1)
    each_hop(lambda hop: send_near(hop, 0))
    each_hop(lambda hop: send_near(hop, 1))
    each_hop(lambda hop: send_far(hop, 1))
    window_copy.wait()
    table_copy.wait()

    ids = [window_ref[assign_ref[ma * groups_here + g]] for g in range(groups_here)]
    for g in range(groups_here):
        for e in range(2):

            def fill(j, c, g=g, e=e):
                start = pl.multiple_of(j * 128, 128)
                table = jnp.concatenate(
                    [
                        leg_ref[g, pl.ds(mine * tail, body), e, pl.ds(start, 128)],
                        leg_ref[g, pl.ds((1 - mine) * body, tail), e, pl.ds(start, 128)],
                    ],
                    axis=0,
                ).astype(F32).T
                k = start + lax.broadcasted_iota(jnp.int32, (128, 1), 0)
                under = 2 * k + e < 2 * kcols - ids[g]
                lower = jnp.where(under, table, 0.0)
                upper = jnp.where(under, 0.0, table)
                weight[g, e, pl.ds(start, 128), :] = jnp.concatenate(
                    [lower[:, :body], upper[:, :body], lower[:, body:], upper[:, body:]],
                    axis=1,
                ).astype(BF16)
                return c

            lax.fori_loop(0, kcols // 128, fill, 0)

    lane = lax.broadcasted_iota(jnp.int32, (1, rows), 1)
    in_upper = ((lane >= body) & (lane < 2 * body)) | (lane >= 2 * body + tail)

    chunks = [(g, j) for j in range(2) for g in range(groups_here)]
    last = len(chunks) - 1

    def remote(c, e, k, source, target, there):
        return pltpu.make_async_remote_copy(
            src_ref=source,
            dst_ref=target,
            send_sem=psend_sem.at[c, e, k],
            recv_sem=precv_sem.at[c, e, k],
            device_id=(there, ma),
            device_id_type=MESH,
        )

    def own_copy(c, e):
        return pltpu.make_async_copy(
            part.at[c, lat, e], out_ref.at[0, c, e], own_sem.at[c, e]
        )

    def beside_copy(c, e):
        return remote(c, e, 0, part.at[c, beside, e], out_ref.at[1, c, e], beside)

    def across_copy(c, e):
        source = part.at[c, across, e]
        if c == last:
            return remote(c, e, 1, source, out_ref.at[3, c, e], across)
        return remote(c, e, 1, source, relay.at[c, e], beside)

    def partner_copy(c, e):
        return remote(c, e, 2, part.at[c, partner, e], out_ref.at[2, c, e], partner)

    def multiply(c):
        g, j = chunks[c]
        h = lax.rem(my_half + j, 2)

        def arrive(m, v):
            for ns in range(2):
                piece = recv.at[g, ns, h * half_ma + m]
                pltpu.make_async_copy(piece, piece, recv_sem.at[g, ns, h * half_ma + m]).wait()
            return v

        lax.fori_loop(0, half_ma, arrive, 0)
        north = recv[g, 0, pl.ds(h * half_ma, half_ma)].reshape(half_f, rows).astype(F32)
        south = recv[g, 1, pl.ds(h * half_ma, half_ma)].reshape(half_f, rows).astype(F32)
        for e in range(2):
            odd = lax.rem(ids[g] + e, 2).astype(F32)
            sign = jnp.where(in_upper, 1.0 - 2.0 * odd, 1.0 - 2.0 * e)
            source = (north + sign * south).astype(BF16)

            def product(d):
                part[c, d, e] = lax.dot_general(
                    weight[g, e, pl.ds(pl.multiple_of(d * block, 16), block), :],
                    source,
                    (((1,), (1,)), ((), ())),
                    preferred_element_type=F32,
                ).astype(BF16)

            product(across)
            across_copy(c, e).start()
            product(beside)
            beside_copy(c, e).start()
            product(partner)
            if c == last:
                partner_copy(c, e).start()
            product(lat)
            own_copy(c, e).start()

    def pass_on(c):
        for e in range(2):
            across_copy(c, e).wait_recv()
            total = part[c, partner, e].astype(F32) + relay[c, e].astype(F32)
            part[c, partner, e] = total.astype(BF16)
            partner_copy(c, e).start()

    for c in range(last + 1):
        multiply(c)
        if 0 < c:
            pass_on(c - 1)

    for c in range(last + 1):
        for e in range(2):
            beside_copy(c, e).wait_recv()
            if c == last:
                across_copy(c, e).wait_recv()
            partner_copy(c, e).wait_recv()

    for g in range(groups_here):

        def sent(q, c, g=g):
            row_copy(g, q, False).wait_send()

            @pl.when(q != ma)
            def _():
                row_copy(g, q, True).wait_send()

            return c

        lax.fori_loop(0, ma_n, sent, 0)
    for c in range(last + 1):
        for e in range(2):
            beside_copy(c, e).wait_send()
            across_copy(c, e).wait_send()
            partner_copy(c, e).wait_send()
            own_copy(c, e).wait()


def sum_kernel(ma_n, parts_ref, out_hbm, held, total, in_sem, out_sem):
    chunk_count = held.shape[1]
    groups_here = chunk_count // 2
    half_f = held.shape[4]
    my_half = lax.axis_index("ma") // (ma_n // 2)

    def fetch(c):
        terms = 4 if c == chunk_count - 1 else 3
        return pltpu.make_async_copy(
            parts_ref.at[pl.ds(0, terms), c], held.at[pl.ds(0, terms), c], in_sem.at[c]
        )

    def store(c):
        at = pl.multiple_of(lax.rem(my_half + c // groups_here, 2) * half_f, 128)
        return pltpu.make_async_copy(
            total.at[c],
            out_hbm.at[c % groups_here, :, :, pl.ds(at, half_f)],
            out_sem.at[c],
        )

    for c in range(chunk_count):
        fetch(c).start()
    for c in range(chunk_count):
        fetch(c).wait()
        value = held[0, c].astype(F32)
        for k in range(1, 4 if c == chunk_count - 1 else 3):
            value = value + held[k, c].astype(F32)
        total[c] = value
        store(c).start()
    for c in range(chunk_count):
        store(c).wait()


def fused_on_device(fourier, legendre, window, assign):
    lat_n, ma_n = lax.axis_size("lat"), lax.axis_size("ma")
    _, slots, fields_here, rows = fourier.shape
    groups_here, pair, parities, kcols = legendre.shape
    block = kcols // lat_n
    fields = fields_here * ma_n
    chunks = 2 * groups_here
    half_f = fields // 2
    hbm = pl.BlockSpec(memory_space=pltpu.HBM)
    anywhere = pl.BlockSpec(memory_space=pl.ANY)
    dma = pltpu.SemaphoreType.DMA
    parts = pl.pallas_call(
        functools.partial(fused_kernel, lat_n, ma_n),
        out_shape=jax.ShapeDtypeStruct((4, chunks, 2, block, half_f), BF16),
        in_specs=[hbm, hbm, hbm, hbm],
        out_specs=anywhere,
        scratch_shapes=[
            pltpu.SMEM(assign.shape, jnp.int32),
            pltpu.SMEM(window.shape, jnp.int32),
            pltpu.VMEM(fourier.shape, BF16),
            pltpu.VMEM(legendre.shape, BF16),
            pltpu.VMEM((groups_here, ma_n, 2, fields_here, rows), BF16),
            pltpu.VMEM((groups_here, 2, ma_n, fields_here, rows), BF16),
            pltpu.VMEM((groups_here, 2, kcols, rows), BF16),
            pltpu.VMEM((chunks, lat_n, 2, block, half_f), BF16),
            pltpu.VMEM((chunks - 1, 2, block, half_f), BF16),
            dma((groups_here, ma_n, 2)),
            dma((groups_here, 2, ma_n)),
            dma((chunks, 2, 3)),
            dma((chunks, 2, 3)),
            dma((chunks, 2)),
            dma((4,)),
            pltpu.SemaphoreType.REGULAR,
        ],
        compiler_params=pltpu.CompilerParams(
            collective_id=0, has_side_effects=True, vmem_limit_bytes=24 * 2**20
        ),
        cost_estimate=pl.CostEstimate(
            flops=8 * groups_here * kcols * rows * fields,
            bytes_accessed=2 * (fourier.size + legendre.size),
            transcendentals=0,
        ),
    )(*(pltpu.with_memory_space_constraint(x, pltpu.HBM) for x in (assign, window, fourier, legendre)))
    return pl.pallas_call(
        functools.partial(sum_kernel, ma_n),
        out_shape=jax.ShapeDtypeStruct((groups_here, 2, block, fields), F32),
        in_specs=[anywhere],
        out_specs=hbm,
        scratch_shapes=[
            pltpu.VMEM(parts.shape, BF16),
            pltpu.VMEM((chunks, 2, block, half_f), F32),
            dma((chunks,)),
            dma((chunks,)),
        ],
        compiler_params=pltpu.CompilerParams(vmem_limit_bytes=16 * 2**20),
        cost_estimate=pl.CostEstimate(
            flops=parts.size, bytes_accessed=4 * parts.size, transcendentals=0
        ),
    )(parts)


def fits_kernel(mesh, fourier, legendre):
    lat_n, ma_n = mesh.shape["lat"], mesh.shape["ma"]
    fields_here = fourier.shape[2] // ma_n
    pair = legendre.shape[1] // lat_n
    block = legendre.shape[3] // lat_n
    return (
        fourier.shape[1] == 2
        and lat_n == 4
        and ma_n == 8
        and legendre.shape[0] == 2 * ma_n
        and fields_here % 16 == 0
        and (fields_here * ma_n) % 256 == 0
        and (2 * pair) % 128 == 0
        and block % 16 == 0
        and legendre.shape[3] % 128 == 0
    )


def solution(mesh):
    def run(fourier, legendre, window, assign):
        fused = fits_kernel(mesh, fourier, legendre)
        return jax.shard_map(
            fused_on_device if fused else plain_on_device,
            mesh=mesh,
            in_specs=(P(None, None, "ma", "lat"), P("ma", "lat", None, None), P(), P()),
            out_specs=P("ma", None, "lat", None),
            check_vma=False,
        )(fourier, legendre, window, assign)

    return run
```

```python
import functools

import jax
import jax.numpy as jnp
from jax import lax
from jax.experimental import pallas as pl
from jax.experimental.pallas import tpu as pltpu
from jax.sharding import PartitionSpec as P

MESH = pl.DeviceIdType.MESH
BF16 = jnp.bfloat16
F32 = jnp.float32


def swapped(value, axis, bit):
    mask = 2**bit
    pairs = [(source, source ^ mask) for source in range(lax.axis_size(axis))]
    return lax.ppermute(value, axis, pairs)


def fold_pairs(latitudes, northern):
    pair_rows = latitudes.shape[3] // 2
    leading_rows = latitudes[:, :, :, :pair_rows]
    trailing_rows = latitudes[:, :, :, pair_rows:]
    outgoing = jnp.where(northern, trailing_rows, leading_rows)
    bit_number = lax.axis_size("lat").bit_length() - 2
    arrived = swapped(outgoing, "lat", bit_number)
    staying = jnp.where(northern, leading_rows, trailing_rows)
    upper_rows = jnp.where(northern, staying, arrived).astype(F32)
    lower_rows = jnp.where(northern, arrived, staying).astype(F32)
    return (
        (upper_rows + lower_rows).astype(BF16),
        (upper_rows - lower_rows).astype(BF16),
    )


def plain_on_device(fourier, legendre, window, assign):
    local_groups = legendre.shape[0]
    lat_count = lax.axis_size("lat")
    northern = lax.axis_index("lat") < lat_count // 2
    count = assign.shape[0]
    chosen = assign[:, None] == lax.iota(jnp.int32, count)[None, :]
    ordered = jnp.einsum(
        "iw,wsfr->isfr", chosen.astype(BF16), fourier, preferred_element_type=F32
    ).astype(BF16)
    gathered = lax.all_to_all(ordered, "ma", split_axis=0, concat_axis=2, tiled=True)
    sym_part, anti_part = fold_pairs(gathered, northern)
    all_ids = jnp.sum(jnp.where(chosen, window[None, :], 0), axis=1)
    group_ids = lax.dynamic_slice_in_dim(
        all_ids, lax.axis_index("ma") * local_groups, local_groups
    )
    column_count = legendre.shape[3]
    wave_total = 2 * column_count
    zero_value = jnp.zeros((), BF16)

    def half_term(parity):
        column = 2 * lax.iota(jnp.int32, column_count) + parity
        upper_slot = (column[None, :] >= wave_total - group_ids[:, None])[:, None, :]
        table_part = legendre[:, :, parity, :]
        masked = jnp.stack(
            [
                jnp.where(upper_slot, zero_value, table_part),
                jnp.where(upper_slot, table_part, zero_value),
            ],
            axis=1,
        )
        leading = sym_part[:, 0] if parity == 0 else anti_part[:, 0]
        flipped = ((group_ids + parity) % 2 == 1)[:, None, None]
        trailing = jnp.where(flipped, anti_part[:, 1], sym_part[:, 1])
        sources = jnp.stack([leading, trailing], axis=1)
        return jnp.einsum("gspk,gsfp->gkf", masked, sources, preferred_element_type=F32)

    partials = jnp.stack([half_term(0), half_term(1)], axis=1)
    return lax.psum_scatter(
        partials.astype(BF16), "lat", scatter_dimension=2, tiled=True
    ).astype(F32)


def fused_kernel(
    lat_n,
    ma_n,
    assign_hbm,
    window_hbm,
    four_hbm,
    leg_hbm,
    out_ref,
    assign_ref,
    window_ref,
    four_ref,
    leg_ref,
    stage,
    recv,
    weight,
    part,
    relay,
    send_sem,
    recv_sem,
    psend_sem,
    precv_sem,
    own_sem,
    load_sem,
    here_sem,
):
    groups_here = leg_ref.shape[0]
    fields_here = four_ref.shape[2]
    rows = four_ref.shape[3]
    pair = rows // 2
    body = pair // 128 * 128
    tail = pair - body
    kcols = leg_ref.shape[3]
    block = kcols // lat_n
    hemi = lat_n // 2
    half_ma = ma_n // 2
    half_f = half_ma * fields_here

    lat = lax.axis_index("lat")
    ma = lax.axis_index("ma")
    side = lat // hemi
    mine = side
    partner = lax.rem(lat + hemi, lat_n)
    my_half = ma // half_ma

    beside = lat + 1 - 2 * lax.rem(lat, 2)
    across = lax.rem(beside + hemi, lat_n)

    assign_copy = pltpu.make_async_copy(assign_hbm, assign_ref, load_sem.at[0])
    window_copy = pltpu.make_async_copy(window_hbm, window_ref, load_sem.at[1])
    rows_copy = pltpu.make_async_copy(four_hbm, four_ref, load_sem.at[2])
    table_copy = pltpu.make_async_copy(leg_hbm, leg_ref, load_sem.at[3])
    assign_copy.start()
    rows_copy.start()

    far = lax.rem(ma + half_ma, ma_n)
    far_first = (1 - my_half) * half_ma
    near_first = my_half * half_ma
    low = lax.rem(ma, 2)

    barrier = pltpu.get_barrier_semaphore()
    met = 0
    for m in range(half_ma):
        for there in (lat, partner):
            pl.semaphore_signal(
                barrier, inc=1, device_id=(there, far_first + m), device_id_type=MESH
            )
            met += 1
    for there in (beside, across):
        pl.semaphore_signal(barrier, inc=1, device_id=(there, far), device_id_type=MESH)
        met += 1
    window_copy.start()
    table_copy.start()

    def pack(q, g):
        slab = four_ref.at[assign_ref[q * groups_here + g]]
        for t in range(2):
            at, rest = t * (pair + tail), body + t * tail
            stage[g, q, t] = jnp.concatenate(
                [slab[n, :, at : at + body] for n in range(2)]
                + [slab[n, :, rest : rest + tail] for n in range(2)],
                axis=1,
            )

    def row_copy(g, q, own):
        t = mine if own else 1 - mine
        return pltpu.make_async_remote_copy(
            src_ref=stage.at[g, q, t],
            dst_ref=recv.at[g, side, ma],
            send_sem=send_sem.at[g, q, t],
            recv_sem=recv_sem.at[g, side, ma],
            device_id=(lat if own else partner, q),
            device_id_type=MESH,
        )

    def place(hop):
        return hop // 2 * 2 + lax.rem(hop + low, 2)

    def send_far(hop, g):
        q = far_first + place(hop)
        pack(q, g)
        row_copy(g, q, False).start()
        row_copy(g, q, True).start()

    def send_near(hop, g):
        q = near_first + place(hop)
        pack(q, g)
        row_copy(g, q, False).start()

        @pl.when(q != ma)
        def _():
            row_copy(g, q, True).start()

        @pl.when(q == ma)
        def _():
            pltpu.make_async_copy(
                stage.at[g, q, mine], recv.at[g, side, ma], recv_sem.at[g, side, ma]
            ).start()

    def each_hop(step):
        def body_of(hop, c):
            step(hop)
            return c

        lax.fori_loop(0, half_ma, body_of, 0)

    assign_copy.wait()
    rows_copy.wait()
    pl.semaphore_wait(barrier, met)
    pl.semaphore_signal(here_sem, inc=1, device_id=(lat, far), device_id_type=MESH)
    each_hop(lambda hop: send_far(hop, 0))
    pl.semaphore_wait(here_sem, 1)
    each_hop(lambda hop: send_near(hop, 0))
    each_hop(lambda hop: send_near(hop, 1))
    each_hop(lambda hop: send_far(hop, 1))
    window_copy.wait()
    table_copy.wait()

    ids = [window_ref[assign_ref[ma * groups_here + g]] for g in range(groups_here)]
    for g in range(groups_here):
        for e in range(2):

            def fill(j, c, g=g, e=e):
                start = pl.multiple_of(j * 128, 128)
                table = jnp.concatenate(
                    [
                        leg_ref[g, pl.ds(mine * tail, body), e, pl.ds(start, 128)],
                        leg_ref[g, pl.ds((1 - mine) * body, tail), e, pl.ds(start, 128)],
                    ],
                    axis=0,
                ).astype(F32).T
                k = start + lax.broadcasted_iota(jnp.int32, (128, 1), 0)
                under = 2 * k + e < 2 * kcols - ids[g]
                lower = jnp.where(under, table, 0.0)
                upper = jnp.where(under, 0.0, table)
                weight[g, e, pl.ds(start, 128), :] = jnp.concatenate(
                    [lower[:, :body], upper[:, :body], lower[:, body:], upper[:, body:]],
                    axis=1,
                ).astype(BF16)
                return c

            lax.fori_loop(0, kcols // 128, fill, 0)

    lane = lax.broadcasted_iota(jnp.int32, (1, rows), 1)
    in_upper = ((lane >= body) & (lane < 2 * body)) | (lane >= 2 * body + tail)

    chunks = [(g, j) for j in range(2) for g in range(groups_here)]
    last = len(chunks) - 1

    def remote(c, e, k, source, target, there):
        return pltpu.make_async_remote_copy(
            src_ref=source,
            dst_ref=target,
            send_sem=psend_sem.at[c, e, k],
            recv_sem=precv_sem.at[c, e, k],
            device_id=(there, ma),
            device_id_type=MESH,
        )

    def own_copy(c, e):
        return pltpu.make_async_copy(
            part.at[c, lat, e], out_ref.at[0, c, e], own_sem.at[c, e]
        )

    def beside_copy(c, e):
        return remote(c, e, 0, part.at[c, beside, e], out_ref.at[1, c, e], beside)

    def across_copy(c, e):
        source = part.at[c, across, e]
        if c == last:
            return remote(c, e, 1, source, out_ref.at[3, c, e], across)
        return remote(c, e, 1, source, relay.at[c, e], beside)

    def partner_copy(c, e):
        return remote(c, e, 2, part.at[c, partner, e], out_ref.at[2, c, e], partner)

    def arrive(g, m):
        for ns in range(2):
            piece = recv.at[g, ns, m]
            pltpu.make_async_copy(piece, piece, recv_sem.at[g, ns, m]).wait()

    def source_of(g, e, north, south):
        odd = lax.rem(ids[g] + e, 2).astype(F32)
        sign = jnp.where(in_upper, 1.0 - 2.0 * odd, 1.0 - 2.0 * e)
        return (north + sign * south).astype(BF16)

    def product(g, e, d, source):
        return lax.dot_general(
            weight[g, e, pl.ds(pl.multiple_of(d * block, 16), block), :],
            source,
            (((1,), (1,)), ((), ())),
            preferred_element_type=F32,
        )

    def send_parts(c, k, value):
        for d in (across, beside, partner, lat):
            part[c, d, k] = value(d).astype(BF16)
            if d is across:
                across_copy(c, k).start()
            elif d is beside:
                beside_copy(c, k).start()
            elif d is lat:
                own_copy(c, k).start()
            elif c == last:
                partner_copy(c, k).start()

    def multiply(c):
        g, j = chunks[c]
        first = lax.rem(my_half + j, 2) * half_ma

        def each(m, v):
            arrive(g, first + m)
            return v

        lax.fori_loop(0, half_ma, each, 0)
        north = recv[g, 0, pl.ds(first, half_ma)].reshape(half_f, rows).astype(F32)
        south = recv[g, 1, pl.ds(first, half_ma)].reshape(half_f, rows).astype(F32)
        for e in range(2):
            source = source_of(g, e, north, south)
            send_parts(c, e, lambda d, e=e, source=source: product(g, e, d, source))

    even_lane = lax.broadcasted_iota(jnp.int32, (1, half_f), 1) < half_f // 2

    def multiply_last():
        g = chunks[last][0]
        for k in range(2):
            core = lax.rem(low + k, 2)
            members = [far_first + 2 * n + core for n in range(half_ma // 2)]
            for m in members:
                arrive(g, m)
            north, south = (
                jnp.concatenate([recv[g, ns, m] for m in members], axis=0).astype(F32)
                for ns in range(2)
            )
            source = jnp.concatenate(
                [source_of(g, e, north, south) for e in range(2)], axis=0
            )
            send_parts(
                last,
                k,
                lambda d, source=source: jnp.where(
                    even_lane, product(g, 0, d, source), product(g, 1, d, source)
                ),
            )

    def pass_on(c):
        for e in range(2):
            across_copy(c, e).wait_recv()
            total = part[c, partner, e].astype(F32) + relay[c, e].astype(F32)
            part[c, partner, e] = total.astype(BF16)
            partner_copy(c, e).start()

    multiply(0)
    multiply(1)
    pass_on(0)
    pass_on(1)
    multiply(2)
    pass_on(2)
    multiply_last()

    for c in range(last + 1):
        for e in range(2):
            beside_copy(c, e).wait_recv()
            if c == last:
                across_copy(c, e).wait_recv()
            partner_copy(c, e).wait_recv()

    for g in range(groups_here):

        def sent(q, c, g=g):
            row_copy(g, q, False).wait_send()

            @pl.when(q != ma)
            def _():
                row_copy(g, q, True).wait_send()

            return c

        lax.fori_loop(0, ma_n, sent, 0)
    for c in range(last + 1):
        for e in range(2):
            beside_copy(c, e).wait_send()
            across_copy(c, e).wait_send()
            partner_copy(c, e).wait_send()
            own_copy(c, e).wait()


def sum_kernel(ma_n, parts_ref, out_hbm, held, total, in_sem, out_sem):
    chunk_count = held.shape[1]
    groups_here = chunk_count // 2
    half_f = held.shape[4]
    my_half = lax.axis_index("ma") // (ma_n // 2)

    def fetch(c):
        terms = 4 if c == chunk_count - 1 else 3
        return pltpu.make_async_copy(
            parts_ref.at[pl.ds(0, terms), c], held.at[pl.ds(0, terms), c], in_sem.at[c]
        )

    def store(c):
        at = pl.multiple_of(lax.rem(my_half + c // groups_here, 2) * half_f, 128)
        return pltpu.make_async_copy(
            total.at[c],
            out_hbm.at[c % groups_here, :, :, pl.ds(at, half_f)],
            out_sem.at[c],
        )

    for c in range(chunk_count):
        fetch(c).start()
    for c in range(chunk_count):
        fetch(c).wait()
        value = held[0, c].astype(F32)
        for k in range(1, 4 if c == chunk_count - 1 else 3):
            value = value + held[k, c].astype(F32)
        if c < chunk_count - 1:
            total[c] = value
        else:
            swap = lax.rem(lax.axis_index("ma"), 2) == 1
            lower = jnp.where(swap, value[1], value[0])
            upper = jnp.where(swap, value[0], value[1])
            width = half_f // 4
            for e in range(2):
                at = 2 * e * width
                total[c, e] = jnp.concatenate(
                    [
                        lower[:, at : at + width],
                        upper[:, at : at + width],
                        lower[:, at + width : at + 2 * width],
                        upper[:, at + width : at + 2 * width],
                    ],
                    axis=1,
                )
        store(c).start()
    for c in range(chunk_count):
        store(c).wait()


def fused_on_device(fourier, legendre, window, assign):
    lat_n, ma_n = lax.axis_size("lat"), lax.axis_size("ma")
    _, slots, fields_here, rows = fourier.shape
    groups_here, pair, parities, kcols = legendre.shape
    block = kcols // lat_n
    fields = fields_here * ma_n
    chunks = 2 * groups_here
    half_f = fields // 2
    hbm = pl.BlockSpec(memory_space=pltpu.HBM)
    anywhere = pl.BlockSpec(memory_space=pl.ANY)
    dma = pltpu.SemaphoreType.DMA
    parts = pl.pallas_call(
        functools.partial(fused_kernel, lat_n, ma_n),
        out_shape=jax.ShapeDtypeStruct((4, chunks, 2, block, half_f), BF16),
        in_specs=[hbm, hbm, hbm, hbm],
        out_specs=anywhere,
        scratch_shapes=[
            pltpu.SMEM(assign.shape, jnp.int32),
            pltpu.SMEM(window.shape, jnp.int32),
            pltpu.VMEM(fourier.shape, BF16),
            pltpu.VMEM(legendre.shape, BF16),
            pltpu.VMEM((groups_here, ma_n, 2, fields_here, rows), BF16),
            pltpu.VMEM((groups_here, 2, ma_n, fields_here, rows), BF16),
            pltpu.VMEM((groups_here, 2, kcols, rows), BF16),
            pltpu.VMEM((chunks, lat_n, 2, block, half_f), BF16),
            pltpu.VMEM((chunks - 1, 2, block, half_f), BF16),
            dma((groups_here, ma_n, 2)),
            dma((groups_here, 2, ma_n)),
            dma((chunks, 2, 3)),
            dma((chunks, 2, 3)),
            dma((chunks, 2)),
            dma((4,)),
            pltpu.SemaphoreType.REGULAR,
        ],
        compiler_params=pltpu.CompilerParams(
            collective_id=0, has_side_effects=True, vmem_limit_bytes=24 * 2**20
        ),
        cost_estimate=pl.CostEstimate(
            flops=8 * groups_here * kcols * rows * fields,
            bytes_accessed=2 * (fourier.size + legendre.size),
            transcendentals=0,
        ),
    )(*(pltpu.with_memory_space_constraint(x, pltpu.HBM) for x in (assign, window, fourier, legendre)))
    return pl.pallas_call(
        functools.partial(sum_kernel, ma_n),
        out_shape=jax.ShapeDtypeStruct((groups_here, 2, block, fields), F32),
        in_specs=[anywhere],
        out_specs=hbm,
        scratch_shapes=[
            pltpu.VMEM(parts.shape, BF16),
            pltpu.VMEM((chunks, 2, block, half_f), F32),
            dma((chunks,)),
            dma((chunks,)),
        ],
        compiler_params=pltpu.CompilerParams(vmem_limit_bytes=16 * 2**20),
        cost_estimate=pl.CostEstimate(
            flops=parts.size, bytes_accessed=4 * parts.size, transcendentals=0
        ),
    )(parts)


def fits_kernel(mesh, fourier, legendre):
    lat_n, ma_n = mesh.shape["lat"], mesh.shape["ma"]
    fields_here = fourier.shape[2] // ma_n
    pair = legendre.shape[1] // lat_n
    block = legendre.shape[3] // lat_n
    return (
        fourier.shape[1] == 2
        and lat_n == 4
        and ma_n == 8
        and legendre.shape[0] == 2 * ma_n
        and fields_here % 16 == 0
        and (fields_here * ma_n) % 256 == 0
        and (2 * pair) % 128 == 0
        and block % 16 == 0
        and legendre.shape[3] % 128 == 0
    )


def solution(mesh):
    def run(fourier, legendre, window, assign):
        fused = fits_kernel(mesh, fourier, legendre)
        return jax.shard_map(
            fused_on_device if fused else plain_on_device,
            mesh=mesh,
            in_specs=(P(None, None, "ma", "lat"), P("ma", "lat", None, None), P(), P()),
            out_specs=P("ma", None, "lat", None),
            check_vma=False,
        )(fourier, legendre, window, assign)

    return run
```

```python
import functools

import jax
import jax.numpy as jnp
from jax import lax
from jax.experimental import pallas as pl
from jax.experimental.pallas import tpu as pltpu
from jax.sharding import PartitionSpec as P

MESH = pl.DeviceIdType.MESH
BF16 = jnp.bfloat16
F32 = jnp.float32


def swapped(value, axis, bit):
    mask = 2**bit
    pairs = [(source, source ^ mask) for source in range(lax.axis_size(axis))]
    return lax.ppermute(value, axis, pairs)


def fold_pairs(latitudes, northern):
    pair_rows = latitudes.shape[3] // 2
    leading_rows = latitudes[:, :, :, :pair_rows]
    trailing_rows = latitudes[:, :, :, pair_rows:]
    outgoing = jnp.where(northern, trailing_rows, leading_rows)
    bit_number = lax.axis_size("lat").bit_length() - 2
    arrived = swapped(outgoing, "lat", bit_number)
    staying = jnp.where(northern, leading_rows, trailing_rows)
    upper_rows = jnp.where(northern, staying, arrived).astype(F32)
    lower_rows = jnp.where(northern, arrived, staying).astype(F32)
    return (
        (upper_rows + lower_rows).astype(BF16),
        (upper_rows - lower_rows).astype(BF16),
    )


def plain_on_device(fourier, legendre, window, assign):
    local_groups = legendre.shape[0]
    lat_count = lax.axis_size("lat")
    northern = lax.axis_index("lat") < lat_count // 2
    count = assign.shape[0]
    chosen = assign[:, None] == lax.iota(jnp.int32, count)[None, :]
    ordered = jnp.einsum(
        "iw,wsfr->isfr", chosen.astype(BF16), fourier, preferred_element_type=F32
    ).astype(BF16)
    gathered = lax.all_to_all(ordered, "ma", split_axis=0, concat_axis=2, tiled=True)
    sym_part, anti_part = fold_pairs(gathered, northern)
    all_ids = jnp.sum(jnp.where(chosen, window[None, :], 0), axis=1)
    group_ids = lax.dynamic_slice_in_dim(
        all_ids, lax.axis_index("ma") * local_groups, local_groups
    )
    column_count = legendre.shape[3]
    wave_total = 2 * column_count
    zero_value = jnp.zeros((), BF16)

    def half_term(parity):
        column = 2 * lax.iota(jnp.int32, column_count) + parity
        upper_slot = (column[None, :] >= wave_total - group_ids[:, None])[:, None, :]
        table_part = legendre[:, :, parity, :]
        masked = jnp.stack(
            [
                jnp.where(upper_slot, zero_value, table_part),
                jnp.where(upper_slot, table_part, zero_value),
            ],
            axis=1,
        )
        leading = sym_part[:, 0] if parity == 0 else anti_part[:, 0]
        flipped = ((group_ids + parity) % 2 == 1)[:, None, None]
        trailing = jnp.where(flipped, anti_part[:, 1], sym_part[:, 1])
        sources = jnp.stack([leading, trailing], axis=1)
        return jnp.einsum("gspk,gsfp->gkf", masked, sources, preferred_element_type=F32)

    partials = jnp.stack([half_term(0), half_term(1)], axis=1)
    return lax.psum_scatter(
        partials.astype(BF16), "lat", scatter_dimension=2, tiled=True
    ).astype(F32)


def fused_kernel(
    lat_n,
    ma_n,
    assign_hbm,
    window_hbm,
    four_hbm,
    leg_hbm,
    sums_ref,
    out_ref,
    assign_ref,
    window_ref,
    four_ref,
    leg_ref,
    stage,
    recv,
    weight,
    part,
    relay,
    landed,
    total,
    send_sem,
    recv_sem,
    psend_sem,
    precv_sem,
    own_sem,
    sum_sem,
    load_sem,
    here_sem,
    late_sem,
):
    groups_here = leg_ref.shape[0]
    fields_here = four_ref.shape[2]
    rows = four_ref.shape[3]
    pair = rows // 2
    body = pair // 128 * 128
    tail = pair - body
    kcols = leg_ref.shape[3]
    block = kcols // lat_n
    hemi = lat_n // 2
    half_ma = ma_n // 2
    half_f = half_ma * fields_here

    lat = lax.axis_index("lat")
    ma = lax.axis_index("ma")
    side = lat // hemi
    mine = side
    partner = lax.rem(lat + hemi, lat_n)
    my_half = ma // half_ma

    beside = lat + 1 - 2 * lax.rem(lat, 2)
    across = lax.rem(beside + hemi, lat_n)

    assign_copy = pltpu.make_async_copy(assign_hbm, assign_ref, load_sem.at[0])
    window_copy = pltpu.make_async_copy(window_hbm, window_ref, load_sem.at[1])
    rows_copy = pltpu.make_async_copy(four_hbm, four_ref, load_sem.at[2])
    table_copy = pltpu.make_async_copy(leg_hbm, leg_ref, load_sem.at[3])
    assign_copy.start()
    rows_copy.start()

    far = lax.rem(ma + half_ma, ma_n)
    far_first = (1 - my_half) * half_ma
    near_first = my_half * half_ma
    low = lax.rem(ma, 2)

    chip = lax.rem(ma // 2, 2)
    facing = far_first + 2 * chip
    other = far_first + 2 * (1 - chip)

    def signal(semaphore, there, q):
        pl.semaphore_signal(semaphore, inc=1, device_id=(there, q), device_id_type=MESH)

    def signal_chip(semaphore, first):
        for m in range(2):
            for there in (lat, partner):
                signal(semaphore, there, first + m)

    def signal_rest(semaphore):
        signal_chip(semaphore, other)
        for there in (beside, across):
            signal(semaphore, there, far)

    barrier = pltpu.get_barrier_semaphore()
    signal_chip(barrier, facing)

    @pl.when(my_half == 0)
    def _():
        signal_rest(barrier)

    window_copy.start()
    table_copy.start()

    def pack(q, g):
        slab = four_ref.at[assign_ref[q * groups_here + g]]
        for t in range(2):
            at, rest = t * (pair + tail), body + t * tail
            stage[g, q, t] = jnp.concatenate(
                [slab[n, :, at : at + body] for n in range(2)]
                + [slab[n, :, rest : rest + tail] for n in range(2)],
                axis=1,
            )

    def row_copy(g, q, own):
        t = mine if own else 1 - mine
        return pltpu.make_async_remote_copy(
            src_ref=stage.at[g, q, t],
            dst_ref=recv.at[g, side, ma],
            send_sem=send_sem.at[g, q, t],
            recv_sem=recv_sem.at[g, side, ma],
            device_id=(lat if own else partner, q),
            device_id_type=MESH,
        )

    def place(hop, turn=0):
        return lax.rem(hop // 2 + turn, 2) * 2 + lax.rem(hop + low, 2)

    def send_far(hop, g):
        q = far_first + place(hop, chip * (1 - my_half) if g == 0 else 0)
        pack(q, g)
        row_copy(g, q, False).start()
        row_copy(g, q, True).start()

    def send_near(hop, g):
        q = near_first + place(hop)
        pack(q, g)
        row_copy(g, q, False).start()

        @pl.when(q != ma)
        def _():
            row_copy(g, q, True).start()

        @pl.when(q == ma)
        def _():
            pltpu.make_async_copy(
                stage.at[g, q, mine], recv.at[g, side, ma], recv_sem.at[g, side, ma]
            ).start()

    def each_hop(step, first=0, end=half_ma):
        def body_of(hop, c):
            step(hop)
            return c

        lax.fori_loop(first, end, body_of, 0)

    pl.semaphore_wait(barrier, 4 + 6 * my_half)

    @pl.when(my_half == 1)
    def _():
        signal_rest(late_sem)
        signal(here_sem, lat, far)

    assign_copy.wait()
    rows_copy.wait()
    each_hop(lambda hop: send_far(hop, 0), 0, half_ma // 2)

    @pl.when(my_half == 0)
    def _():
        pl.semaphore_wait(late_sem, 6)
        signal(here_sem, lat, far)

    pl.semaphore_wait(here_sem, 1)
    each_hop(lambda hop: send_near(hop, 0))
    each_hop(lambda hop: send_far(hop, 0), half_ma // 2)
    each_hop(lambda hop: send_near(hop, 1))
    each_hop(lambda hop: send_far(hop, 1))
    window_copy.wait()
    table_copy.wait()

    ids = [window_ref[assign_ref[ma * groups_here + g]] for g in range(groups_here)]
    for g in range(groups_here):
        for e in range(2):

            def fill(j, c, g=g, e=e):
                start = pl.multiple_of(j * 128, 128)
                table = jnp.concatenate(
                    [
                        leg_ref[g, pl.ds(mine * tail, body), e, pl.ds(start, 128)],
                        leg_ref[g, pl.ds((1 - mine) * body, tail), e, pl.ds(start, 128)],
                    ],
                    axis=0,
                ).astype(F32).T
                k = start + lax.broadcasted_iota(jnp.int32, (128, 1), 0)
                under = 2 * k + e < 2 * kcols - ids[g]
                lower = jnp.where(under, table, 0.0)
                upper = jnp.where(under, 0.0, table)
                weight[g, e, pl.ds(start, 128), :] = jnp.concatenate(
                    [lower[:, :body], upper[:, :body], lower[:, body:], upper[:, body:]],
                    axis=1,
                ).astype(BF16)
                return c

            lax.fori_loop(0, kcols // 128, fill, 0)

    lane = lax.broadcasted_iota(jnp.int32, (1, rows), 1)
    in_upper = ((lane >= body) & (lane < 2 * body)) | (lane >= 2 * body + tail)

    chunks = [(g, j) for j in range(2) for g in range(groups_here)]
    last = len(chunks) - 1

    def remote(c, e, k, source, target, there):
        return pltpu.make_async_remote_copy(
            src_ref=source,
            dst_ref=target,
            send_sem=psend_sem.at[c, e, k],
            recv_sem=precv_sem.at[c, e, k],
            device_id=(there, ma),
            device_id_type=MESH,
        )

    def own_copy(k):
        return pltpu.make_async_copy(part.at[last, lat, k], out_ref.at[0, k], own_sem.at[k])

    def beside_copy(c, e):
        target = out_ref.at[1, e] if c == last else landed.at[0, c, e]
        return remote(c, e, 0, part.at[c, beside, e], target, beside)

    def across_copy(c, e):
        source = part.at[c, across, e]
        if c == last:
            return remote(c, e, 1, source, out_ref.at[3, e], across)
        return remote(c, e, 1, source, relay.at[c, e], beside)

    def partner_copy(c, e):
        target = out_ref.at[2, e] if c == last else landed.at[1, c, e]
        return remote(c, e, 2, part.at[c, partner, e], target, partner)

    def sum_copy(c):
        return pltpu.make_async_copy(total.at[c], sums_ref.at[c], sum_sem.at[c])

    def arrive(g, m):
        for ns in range(2):
            piece = recv.at[g, ns, m]
            pltpu.make_async_copy(piece, piece, recv_sem.at[g, ns, m]).wait()

    def source_of(g, e, north, south):
        odd = lax.rem(ids[g] + e, 2).astype(F32)
        sign = jnp.where(in_upper, 1.0 - 2.0 * odd, 1.0 - 2.0 * e)
        return (north + sign * south).astype(BF16)

    def product(g, e, d, source):
        return lax.dot_general(
            weight[g, e, pl.ds(pl.multiple_of(d * block, 16), block), :],
            source,
            (((1,), (1,)), ((), ())),
            preferred_element_type=F32,
        )

    def send_parts(c, k, value):
        for d in (across, beside, partner, lat):
            part[c, d, k] = value(d).astype(BF16)
            if d is across:
                across_copy(c, k).start()
            elif d is beside:
                beside_copy(c, k).start()
            elif c == last and d is partner:
                partner_copy(c, k).start()
            elif c == last:
                own_copy(k).start()

    def multiply(c):
        g, j = chunks[c]
        first = lax.rem(my_half + j, 2) * half_ma

        def each(m, v):
            arrive(g, first + m)
            return v

        lax.fori_loop(0, half_ma, each, 0)
        north = recv[g, 0, pl.ds(first, half_ma)].reshape(half_f, rows).astype(F32)
        south = recv[g, 1, pl.ds(first, half_ma)].reshape(half_f, rows).astype(F32)
        for e in range(2):
            source = source_of(g, e, north, south)
            send_parts(c, e, lambda d, e=e, source=source: product(g, e, d, source))

    even_lane = lax.broadcasted_iota(jnp.int32, (1, half_f), 1) < half_f // 2

    def multiply_last(k):
        g = chunks[last][0]
        chips = half_ma // 2
        first = far_first + chips * (1 - my_half if k == 0 else my_half)
        for m in range(chips):
            arrive(g, first + m)
        north, south = (
            recv[g, ns, pl.ds(first, chips)].reshape(half_f // 2, rows).astype(F32)
            for ns in range(2)
        )
        source = jnp.concatenate([source_of(g, e, north, south) for e in range(2)], axis=0)
        send_parts(
            last,
            k,
            lambda d: jnp.where(
                even_lane, product(g, 0, d, source), product(g, 1, d, source)
            ),
        )

    def pass_on(c):
        for e in range(2):
            across_copy(c, e).wait_recv()
            total = part[c, partner, e].astype(F32) + relay[c, e].astype(F32)
            part[c, partner, e] = total.astype(BF16)
            partner_copy(c, e).start()

    def finish(c):
        for e in range(2):
            beside_copy(c, e).wait_recv()
            partner_copy(c, e).wait_recv()
            total[c, e] = (
                part[c, lat, e].astype(F32)
                + landed[0, c, e].astype(F32)
                + landed[1, c, e].astype(F32)
            )
        sum_copy(c).start()

    multiply(0)
    multiply(2)
    pass_on(0)
    multiply(1)
    pass_on(2)
    multiply_last(0)
    finish(0)
    pass_on(1)
    finish(2)
    multiply_last(1)
    finish(1)
    for k in range(2):
        beside_copy(last, k).wait_recv()
        across_copy(last, k).wait_recv()
        partner_copy(last, k).wait_recv()

    for g in range(groups_here):

        def sent(q, c, g=g):
            row_copy(g, q, False).wait_send()

            @pl.when(q != ma)
            def _():
                row_copy(g, q, True).wait_send()

            return c

        lax.fori_loop(0, ma_n, sent, 0)
    for c in range(last + 1):
        for e in range(2):
            beside_copy(c, e).wait_send()
            across_copy(c, e).wait_send()
            partner_copy(c, e).wait_send()
    for c in range(last):
        sum_copy(c).wait()
    for k in range(2):
        own_copy(k).wait()


def sum_kernel(ma_n, sums_ref, parts_ref, out_hbm, held, total, in_sem, out_sem):
    last = sums_ref.shape[0]
    groups_here = (last + 1) // 2
    half_f = held.shape[3]
    my_half = lax.axis_index("ma") // (ma_n // 2)

    def store(c):
        at = pl.multiple_of(lax.rem(my_half + c // groups_here, 2) * half_f, 128)
        return pltpu.make_async_copy(
            total if c == last else sums_ref.at[c],
            out_hbm.at[c % groups_here, :, :, pl.ds(at, half_f)],
            out_sem.at[c],
        )

    fetch = pltpu.make_async_copy(parts_ref, held, in_sem)
    fetch.start()
    for c in range(last):
        store(c).start()
    fetch.wait()
    first, second = (
        held[0, k].astype(F32)
        + held[1, k].astype(F32)
        + held[2, k].astype(F32)
        + held[3, k].astype(F32)
        for k in range(2)
    )
    lower = jnp.where(my_half == 0, second, first)
    upper = jnp.where(my_half == 0, first, second)
    width = half_f // 2
    for e in range(2):
        at = e * width
        total[e] = jnp.concatenate(
            [lower[:, at : at + width], upper[:, at : at + width]], axis=1
        )
    store(last).start()
    for c in range(last + 1):
        store(c).wait()


def fused_on_device(fourier, legendre, window, assign):
    lat_n, ma_n = lax.axis_size("lat"), lax.axis_size("ma")
    _, slots, fields_here, rows = fourier.shape
    groups_here, pair, parities, kcols = legendre.shape
    block = kcols // lat_n
    fields = fields_here * ma_n
    chunks = 2 * groups_here
    half_f = fields // 2
    hbm = pl.BlockSpec(memory_space=pltpu.HBM)
    anywhere = pl.BlockSpec(memory_space=pl.ANY)
    dma = pltpu.SemaphoreType.DMA
    sums, parts = pl.pallas_call(
        functools.partial(fused_kernel, lat_n, ma_n),
        out_shape=(
            jax.ShapeDtypeStruct((chunks - 1, 2, block, half_f), F32),
            jax.ShapeDtypeStruct((4, 2, block, half_f), BF16),
        ),
        in_specs=[hbm, hbm, hbm, hbm],
        out_specs=(anywhere, anywhere),
        scratch_shapes=[
            pltpu.SMEM(assign.shape, jnp.int32),
            pltpu.SMEM(window.shape, jnp.int32),
            pltpu.VMEM(fourier.shape, BF16),
            pltpu.VMEM(legendre.shape, BF16),
            pltpu.VMEM((groups_here, ma_n, 2, fields_here, rows), BF16),
            pltpu.VMEM((groups_here, 2, ma_n, fields_here, rows), BF16),
            pltpu.VMEM((groups_here, 2, kcols, rows), BF16),
            pltpu.VMEM((chunks, lat_n, 2, block, half_f), BF16),
            pltpu.VMEM((chunks - 1, 2, block, half_f), BF16),
            pltpu.VMEM((2, chunks - 1, 2, block, half_f), BF16),
            pltpu.VMEM((chunks - 1, 2, block, half_f), F32),
            dma((groups_here, ma_n, 2)),
            dma((groups_here, 2, ma_n)),
            dma((chunks, 2, 3)),
            dma((chunks, 2, 3)),
            dma((2,)),
            dma((chunks - 1,)),
            dma((4,)),
            pltpu.SemaphoreType.REGULAR,
            pltpu.SemaphoreType.REGULAR,
        ],
        compiler_params=pltpu.CompilerParams(
            collective_id=0, has_side_effects=True, vmem_limit_bytes=24 * 2**20
        ),
        cost_estimate=pl.CostEstimate(
            flops=8 * groups_here * kcols * rows * fields,
            bytes_accessed=2 * (fourier.size + legendre.size),
            transcendentals=0,
        ),
    )(*(pltpu.with_memory_space_constraint(x, pltpu.HBM) for x in (assign, window, fourier, legendre)))
    return pl.pallas_call(
        functools.partial(sum_kernel, ma_n),
        out_shape=jax.ShapeDtypeStruct((groups_here, 2, block, fields), F32),
        in_specs=[anywhere, anywhere],
        out_specs=hbm,
        scratch_shapes=[
            pltpu.VMEM(parts.shape, BF16),
            pltpu.VMEM((2, block, half_f), F32),
            dma,
            dma((chunks,)),
        ],
        compiler_params=pltpu.CompilerParams(vmem_limit_bytes=16 * 2**20),
        cost_estimate=pl.CostEstimate(
            flops=parts.size, bytes_accessed=4 * parts.size, transcendentals=0
        ),
    )(sums, parts)


def fits_kernel(mesh, fourier, legendre):
    lat_n, ma_n = mesh.shape["lat"], mesh.shape["ma"]
    fields_here = fourier.shape[2] // ma_n
    pair = legendre.shape[1] // lat_n
    block = legendre.shape[3] // lat_n
    return (
        fourier.shape[1] == 2
        and lat_n == 4
        and ma_n == 8
        and legendre.shape[0] == 2 * ma_n
        and fields_here % 16 == 0
        and (fields_here * ma_n) % 256 == 0
        and (2 * pair) % 128 == 0
        and block % 16 == 0
        and legendre.shape[3] % 128 == 0
    )


def solution(mesh):
    def run(fourier, legendre, window, assign):
        fused = fits_kernel(mesh, fourier, legendre)
        return jax.shard_map(
            fused_on_device if fused else plain_on_device,
            mesh=mesh,
            in_specs=(P(None, None, "ma", "lat"), P("ma", "lat", None, None), P(), P()),
            out_specs=P("ma", None, "lat", None),
            check_vma=False,
        )(fourier, legendre, window, assign)

    return run
```

```python
import functools

import jax
import jax.numpy as jnp
from jax import lax
from jax.experimental import pallas as pl
from jax.experimental.pallas import tpu as pltpu
from jax.sharding import PartitionSpec as P

MESH = pl.DeviceIdType.MESH
BF16 = jnp.bfloat16
F32 = jnp.float32


def swapped(value, axis, bit):
    mask = 2**bit
    pairs = [(source, source ^ mask) for source in range(lax.axis_size(axis))]
    return lax.ppermute(value, axis, pairs)


def fold_pairs(latitudes, northern):
    pair_rows = latitudes.shape[3] // 2
    leading_rows = latitudes[:, :, :, :pair_rows]
    trailing_rows = latitudes[:, :, :, pair_rows:]
    outgoing = jnp.where(northern, trailing_rows, leading_rows)
    bit_number = lax.axis_size("lat").bit_length() - 2
    arrived = swapped(outgoing, "lat", bit_number)
    staying = jnp.where(northern, leading_rows, trailing_rows)
    upper_rows = jnp.where(northern, staying, arrived).astype(F32)
    lower_rows = jnp.where(northern, arrived, staying).astype(F32)
    return (
        (upper_rows + lower_rows).astype(BF16),
        (upper_rows - lower_rows).astype(BF16),
    )


def plain_on_device(fourier, legendre, window, assign):
    local_groups = legendre.shape[0]
    lat_count = lax.axis_size("lat")
    northern = lax.axis_index("lat") < lat_count // 2
    count = assign.shape[0]
    chosen = assign[:, None] == lax.iota(jnp.int32, count)[None, :]
    ordered = jnp.einsum(
        "iw,wsfr->isfr", chosen.astype(BF16), fourier, preferred_element_type=F32
    ).astype(BF16)
    gathered = lax.all_to_all(ordered, "ma", split_axis=0, concat_axis=2, tiled=True)
    sym_part, anti_part = fold_pairs(gathered, northern)
    all_ids = jnp.sum(jnp.where(chosen, window[None, :], 0), axis=1)
    group_ids = lax.dynamic_slice_in_dim(
        all_ids, lax.axis_index("ma") * local_groups, local_groups
    )
    column_count = legendre.shape[3]
    wave_total = 2 * column_count
    zero_value = jnp.zeros((), BF16)

    def half_term(parity):
        column = 2 * lax.iota(jnp.int32, column_count) + parity
        upper_slot = (column[None, :] >= wave_total - group_ids[:, None])[:, None, :]
        table_part = legendre[:, :, parity, :]
        masked = jnp.stack(
            [
                jnp.where(upper_slot, zero_value, table_part),
                jnp.where(upper_slot, table_part, zero_value),
            ],
            axis=1,
        )
        leading = sym_part[:, 0] if parity == 0 else anti_part[:, 0]
        flipped = ((group_ids + parity) % 2 == 1)[:, None, None]
        trailing = jnp.where(flipped, anti_part[:, 1], sym_part[:, 1])
        sources = jnp.stack([leading, trailing], axis=1)
        return jnp.einsum("gspk,gsfp->gkf", masked, sources, preferred_element_type=F32)

    partials = jnp.stack([half_term(0), half_term(1)], axis=1)
    return lax.psum_scatter(
        partials.astype(BF16), "lat", scatter_dimension=2, tiled=True
    ).astype(F32)


def fused_kernel(
    lat_n,
    ma_n,
    assign_hbm,
    window_hbm,
    four_hbm,
    leg_hbm,
    sums_ref,
    out_ref,
    assign_ref,
    window_ref,
    four_ref,
    leg_ref,
    stage,
    recv,
    weight,
    part,
    relay,
    landed,
    total,
    send_sem,
    recv_sem,
    psend_sem,
    precv_sem,
    own_sem,
    sum_sem,
    load_sem,
    here_sem,
    late_sem,
):
    groups_here = leg_ref.shape[0]
    fields_here = four_ref.shape[2]
    rows = four_ref.shape[3]
    pair = rows // 2
    body = pair // 128 * 128
    tail = pair - body
    kcols = leg_ref.shape[3]
    block = kcols // lat_n
    hemi = lat_n // 2
    half_ma = ma_n // 2
    half_f = half_ma * fields_here

    lat = lax.axis_index("lat")
    ma = lax.axis_index("ma")
    side = lat // hemi
    mine = side
    partner = lax.rem(lat + hemi, lat_n)
    my_half = ma // half_ma

    beside = lat + 1 - 2 * lax.rem(lat, 2)
    across = lax.rem(beside + hemi, lat_n)

    assign_copy = pltpu.make_async_copy(assign_hbm, assign_ref, load_sem.at[0])
    window_copy = pltpu.make_async_copy(window_hbm, window_ref, load_sem.at[1])
    rows_copy = pltpu.make_async_copy(four_hbm, four_ref, load_sem.at[2])
    table_copy = pltpu.make_async_copy(leg_hbm, leg_ref, load_sem.at[3])
    assign_copy.start()
    rows_copy.start()

    far_first = (1 - my_half) * half_ma
    near_first = my_half * half_ma
    low = lax.rem(ma, 2)

    chip = lax.rem(ma // 2, 2)
    facing = far_first + 2 * (1 - chip)
    other = far_first + 2 * chip
    far = facing + low

    def signal(semaphore, there, q):
        pl.semaphore_signal(semaphore, inc=1, device_id=(there, q), device_id_type=MESH)

    def signal_chip(semaphore, first):
        for m in range(2):
            for there in (lat, partner):
                signal(semaphore, there, first + m)

    def signal_rest(semaphore):
        signal_chip(semaphore, other)
        for there in (beside, across):
            signal(semaphore, there, far)

    barrier = pltpu.get_barrier_semaphore()
    signal_chip(barrier, facing)

    @pl.when(my_half == 0)
    def _():
        signal_rest(barrier)

    window_copy.start()
    table_copy.start()

    def pack(q, g):
        slab = four_ref.at[assign_ref[q * groups_here + g]]
        for t in range(2):
            at, rest = t * (pair + tail), body + t * tail
            stage[g, q, t] = jnp.concatenate(
                [slab[n, :, at : at + body] for n in range(2)]
                + [slab[n, :, rest : rest + tail] for n in range(2)],
                axis=1,
            )

    def row_copy(g, q, own):
        t = mine if own else 1 - mine
        return pltpu.make_async_remote_copy(
            src_ref=stage.at[g, q, t],
            dst_ref=recv.at[g, side, ma],
            send_sem=send_sem.at[g, q, t],
            recv_sem=recv_sem.at[g, side, ma],
            device_id=(lat if own else partner, q),
            device_id_type=MESH,
        )

    def place(hop, turn=0):
        return lax.rem(hop // 2 + turn, 2) * 2 + lax.rem(hop + low, 2)

    def send_far(hop, g):
        q = far_first + place(hop, (1 - chip) * (1 - my_half) if g == 0 else 0)
        pack(q, g)
        row_copy(g, q, False).start()
        row_copy(g, q, True).start()

    def send_near(hop, g):
        q = near_first + place(hop)
        pack(q, g)
        row_copy(g, q, False).start()

        @pl.when(q != ma)
        def _():
            row_copy(g, q, True).start()

        @pl.when(q == ma)
        def _():
            pltpu.make_async_copy(
                stage.at[g, q, mine], recv.at[g, side, ma], recv_sem.at[g, side, ma]
            ).start()

    def each_hop(step, first=0, end=half_ma):
        def body_of(hop, c):
            step(hop)
            return c

        lax.fori_loop(first, end, body_of, 0)

    pl.semaphore_wait(barrier, 4 + 6 * my_half)

    @pl.when(my_half == 1)
    def _():
        signal_rest(late_sem)
        signal(here_sem, lat, far)

    assign_copy.wait()
    rows_copy.wait()
    each_hop(lambda hop: send_far(hop, 0), 0, half_ma // 2)

    @pl.when(my_half == 0)
    def _():
        pl.semaphore_wait(late_sem, 6)
        signal(here_sem, lat, far)

    pl.semaphore_wait(here_sem, 1)
    each_hop(lambda hop: send_near(hop, 0))
    each_hop(lambda hop: send_far(hop, 0), half_ma // 2)
    each_hop(lambda hop: send_near(hop, 1))
    each_hop(lambda hop: send_far(hop, 1))
    window_copy.wait()
    table_copy.wait()

    ids = [window_ref[assign_ref[ma * groups_here + g]] for g in range(groups_here)]
    for g in range(groups_here):
        for e in range(2):

            def fill(j, c, g=g, e=e):
                start = pl.multiple_of(j * 128, 128)
                table = jnp.concatenate(
                    [
                        leg_ref[g, pl.ds(mine * tail, body), e, pl.ds(start, 128)],
                        leg_ref[g, pl.ds((1 - mine) * body, tail), e, pl.ds(start, 128)],
                    ],
                    axis=0,
                ).astype(F32).T
                k = start + lax.broadcasted_iota(jnp.int32, (128, 1), 0)
                under = 2 * k + e < 2 * kcols - ids[g]
                lower = jnp.where(under, table, 0.0)
                upper = jnp.where(under, 0.0, table)
                weight[g, e, pl.ds(start, 128), :] = jnp.concatenate(
                    [lower[:, :body], upper[:, :body], lower[:, body:], upper[:, body:]],
                    axis=1,
                ).astype(BF16)
                return c

            lax.fori_loop(0, kcols // 128, fill, 0)

    lane = lax.broadcasted_iota(jnp.int32, (1, rows), 1)
    in_upper = ((lane >= body) & (lane < 2 * body)) | (lane >= 2 * body + tail)

    chunks = [(g, j) for j in range(2) for g in range(groups_here)]
    last = len(chunks) - 1

    def remote(c, e, k, source, target, there):
        return pltpu.make_async_remote_copy(
            src_ref=source,
            dst_ref=target,
            send_sem=psend_sem.at[c, e, k],
            recv_sem=precv_sem.at[c, e, k],
            device_id=(there, ma),
            device_id_type=MESH,
        )

    def own_copy(k):
        return pltpu.make_async_copy(part.at[last, lat, k], out_ref.at[0, k], own_sem.at[k])

    def beside_copy(c, e):
        target = out_ref.at[1, e] if c == last else landed.at[0, c, e]
        return remote(c, e, 0, part.at[c, beside, e], target, beside)

    def across_copy(c, e):
        source = part.at[c, across, e]
        if c == last:
            return remote(c, e, 1, source, out_ref.at[3, e], across)
        return remote(c, e, 1, source, relay.at[c, e], beside)

    def partner_copy(c, e):
        target = out_ref.at[2, e] if c == last else landed.at[1, c, e]
        return remote(c, e, 2, part.at[c, partner, e], target, partner)

    def sum_copy(c):
        return pltpu.make_async_copy(total.at[c], sums_ref.at[c], sum_sem.at[c])

    def arrive(g, m):
        for ns in range(2):
            piece = recv.at[g, ns, m]
            pltpu.make_async_copy(piece, piece, recv_sem.at[g, ns, m]).wait()

    def source_of(g, e, north, south):
        odd = lax.rem(ids[g] + e, 2).astype(F32)
        sign = jnp.where(in_upper, 1.0 - 2.0 * odd, 1.0 - 2.0 * e)
        return (north + sign * south).astype(BF16)

    def product(g, e, d, source):
        return lax.dot_general(
            weight[g, e, pl.ds(pl.multiple_of(d * block, 16), block), :],
            source,
            (((1,), (1,)), ((), ())),
            preferred_element_type=F32,
        )

    def send_parts(c, k, value):
        for d in (across, beside, partner, lat):
            part[c, d, k] = value(d).astype(BF16)
            if d is across:
                across_copy(c, k).start()
            elif d is beside:
                beside_copy(c, k).start()
            elif c == last and d is partner:
                partner_copy(c, k).start()
            elif c == last:
                own_copy(k).start()

    def multiply(c):
        g, j = chunks[c]
        first = lax.rem(my_half + j, 2) * half_ma

        def each(m, v):
            arrive(g, first + m)
            return v

        lax.fori_loop(0, half_ma, each, 0)
        north = recv[g, 0, pl.ds(first, half_ma)].reshape(half_f, rows).astype(F32)
        south = recv[g, 1, pl.ds(first, half_ma)].reshape(half_f, rows).astype(F32)
        for e in range(2):
            source = source_of(g, e, north, south)
            send_parts(c, e, lambda d, e=e, source=source: product(g, e, d, source))

    even_lane = lax.broadcasted_iota(jnp.int32, (1, half_f), 1) < half_f // 2

    def multiply_last(k):
        g = chunks[last][0]
        chips = half_ma // 2
        first = far_first + chips * (1 - my_half if k == 0 else my_half)
        for m in range(chips):
            arrive(g, first + m)
        north, south = (
            recv[g, ns, pl.ds(first, chips)].reshape(half_f // 2, rows).astype(F32)
            for ns in range(2)
        )
        source = jnp.concatenate([source_of(g, e, north, south) for e in range(2)], axis=0)
        send_parts(
            last,
            k,
            lambda d: jnp.where(
                even_lane, product(g, 0, d, source), product(g, 1, d, source)
            ),
        )

    def pass_on(c):
        for e in range(2):
            across_copy(c, e).wait_recv()
            total = part[c, partner, e].astype(F32) + relay[c, e].astype(F32)
            part[c, partner, e] = total.astype(BF16)
            partner_copy(c, e).start()

    def finish(c):
        for e in range(2):
            beside_copy(c, e).wait_recv()
            partner_copy(c, e).wait_recv()
            total[c, e] = (
                part[c, lat, e].astype(F32)
                + landed[0, c, e].astype(F32)
                + landed[1, c, e].astype(F32)
            )
        sum_copy(c).start()

    multiply(0)
    multiply(2)
    pass_on(0)
    multiply(1)
    pass_on(2)
    multiply_last(0)
    finish(0)
    pass_on(1)
    finish(2)
    multiply_last(1)
    finish(1)
    for g in range(groups_here):

        def sent(q, c, g=g):
            row_copy(g, q, False).wait_send()

            @pl.when(q != ma)
            def _():
                row_copy(g, q, True).wait_send()

            return c

        lax.fori_loop(0, ma_n, sent, 0)
    for c in range(last):
        for e in range(2):
            beside_copy(c, e).wait_send()
            across_copy(c, e).wait_send()
            partner_copy(c, e).wait_send()
        sum_copy(c).wait()
    for k in range(2):
        own_copy(k).wait()
        beside_copy(last, k).wait()
        across_copy(last, k).wait()
        partner_copy(last, k).wait()


def sum_kernel(ma_n, sums_ref, held, out_hbm, total, out_sem):
    last = sums_ref.shape[0]
    groups_here = (last + 1) // 2
    half_f = held.shape[3]
    my_half = lax.axis_index("ma") // (ma_n // 2)

    def store(c):
        at = pl.multiple_of(lax.rem(my_half + c // groups_here, 2) * half_f, 128)
        return pltpu.make_async_copy(
            total if c == last else sums_ref.at[c],
            out_hbm.at[c % groups_here, :, :, pl.ds(at, half_f)],
            out_sem.at[c],
        )

    for c in range(last):
        store(c).start()
    first, second = (
        held[0, k].astype(F32)
        + held[1, k].astype(F32)
        + held[2, k].astype(F32)
        + held[3, k].astype(F32)
        for k in range(2)
    )
    lower = jnp.where(my_half == 0, second, first)
    upper = jnp.where(my_half == 0, first, second)
    width = half_f // 2
    for e in range(2):
        at = e * width
        total[e] = jnp.concatenate(
            [lower[:, at : at + width], upper[:, at : at + width]], axis=1
        )
    store(last).start()
    for c in range(last + 1):
        store(c).wait()


def fused_on_device(fourier, legendre, window, assign):
    lat_n, ma_n = lax.axis_size("lat"), lax.axis_size("ma")
    _, slots, fields_here, rows = fourier.shape
    groups_here, pair, parities, kcols = legendre.shape
    block = kcols // lat_n
    fields = fields_here * ma_n
    chunks = 2 * groups_here
    half_f = fields // 2
    hbm = pl.BlockSpec(memory_space=pltpu.HBM)
    anywhere = pl.BlockSpec(memory_space=pl.ANY)
    dma = pltpu.SemaphoreType.DMA
    sums, parts = pl.pallas_call(
        functools.partial(fused_kernel, lat_n, ma_n),
        out_shape=(
            jax.ShapeDtypeStruct((chunks - 1, 2, block, half_f), F32),
            jax.ShapeDtypeStruct((4, 2, block, half_f), BF16),
        ),
        in_specs=[hbm, hbm, hbm, hbm],
        out_specs=(anywhere, anywhere),
        scratch_shapes=[
            pltpu.SMEM(assign.shape, jnp.int32),
            pltpu.SMEM(window.shape, jnp.int32),
            pltpu.VMEM(fourier.shape, BF16),
            pltpu.VMEM(legendre.shape, BF16),
            pltpu.VMEM((groups_here, ma_n, 2, fields_here, rows), BF16),
            pltpu.VMEM((groups_here, 2, ma_n, fields_here, rows), BF16),
            pltpu.VMEM((groups_here, 2, kcols, rows), BF16),
            pltpu.VMEM((chunks, lat_n, 2, block, half_f), BF16),
            pltpu.VMEM((chunks - 1, 2, block, half_f), BF16),
            pltpu.VMEM((2, chunks - 1, 2, block, half_f), BF16),
            pltpu.VMEM((chunks - 1, 2, block, half_f), F32),
            dma((groups_here, ma_n, 2)),
            dma((groups_here, 2, ma_n)),
            dma((chunks, 2, 3)),
            dma((chunks, 2, 3)),
            dma((2,)),
            dma((chunks - 1,)),
            dma((4,)),
            pltpu.SemaphoreType.REGULAR,
            pltpu.SemaphoreType.REGULAR,
        ],
        compiler_params=pltpu.CompilerParams(
            collective_id=0, has_side_effects=True, vmem_limit_bytes=24 * 2**20
        ),
        cost_estimate=pl.CostEstimate(
            flops=8 * groups_here * kcols * rows * fields,
            bytes_accessed=2 * (fourier.size + legendre.size),
            transcendentals=0,
        ),
    )(*(pltpu.with_memory_space_constraint(x, pltpu.HBM) for x in (assign, window, fourier, legendre)))
    return pl.pallas_call(
        functools.partial(sum_kernel, ma_n),
        out_shape=jax.ShapeDtypeStruct((groups_here, 2, block, fields), F32),
        in_specs=[anywhere, pl.BlockSpec(memory_space=pltpu.VMEM)],
        out_specs=hbm,
        scratch_shapes=[
            pltpu.VMEM((2, block, half_f), F32),
            dma((chunks,)),
        ],
        compiler_params=pltpu.CompilerParams(vmem_limit_bytes=16 * 2**20),
        cost_estimate=pl.CostEstimate(
            flops=parts.size, bytes_accessed=4 * parts.size, transcendentals=0
        ),
    )(sums, parts)


def fits_kernel(mesh, fourier, legendre):
    lat_n, ma_n = mesh.shape["lat"], mesh.shape["ma"]
    fields_here = fourier.shape[2] // ma_n
    pair = legendre.shape[1] // lat_n
    block = legendre.shape[3] // lat_n
    return (
        fourier.shape[1] == 2
        and lat_n == 4
        and ma_n == 8
        and legendre.shape[0] == 2 * ma_n
        and fields_here % 16 == 0
        and (fields_here * ma_n) % 256 == 0
        and (2 * pair) % 128 == 0
        and block % 16 == 0
        and legendre.shape[3] % 128 == 0
    )


def solution(mesh):
    def run(fourier, legendre, window, assign):
        fused = fits_kernel(mesh, fourier, legendre)
        return jax.shard_map(
            fused_on_device if fused else plain_on_device,
            mesh=mesh,
            in_specs=(P(None, None, "ma", "lat"), P("ma", "lat", None, None), P(), P()),
            out_specs=P("ma", None, "lat", None),
            check_vma=False,
        )(fourier, legendre, window, assign)

    return run
```

```python
import functools

import jax
import jax.numpy as jnp
from jax import lax
from jax.experimental import pallas as pl
from jax.experimental.pallas import tpu as pltpu
from jax.sharding import PartitionSpec as P

MESH = pl.DeviceIdType.MESH
BF16 = jnp.bfloat16
F32 = jnp.float32


def swapped(value, axis, bit):
    mask = 2**bit
    pairs = [(source, source ^ mask) for source in range(lax.axis_size(axis))]
    return lax.ppermute(value, axis, pairs)


def fold_pairs(latitudes, northern):
    pair_rows = latitudes.shape[3] // 2
    leading_rows = latitudes[:, :, :, :pair_rows]
    trailing_rows = latitudes[:, :, :, pair_rows:]
    outgoing = jnp.where(northern, trailing_rows, leading_rows)
    bit_number = lax.axis_size("lat").bit_length() - 2
    arrived = swapped(outgoing, "lat", bit_number)
    staying = jnp.where(northern, leading_rows, trailing_rows)
    upper_rows = jnp.where(northern, staying, arrived).astype(F32)
    lower_rows = jnp.where(northern, arrived, staying).astype(F32)
    return (
        (upper_rows + lower_rows).astype(BF16),
        (upper_rows - lower_rows).astype(BF16),
    )


def plain_on_device(fourier, legendre, window, assign):
    local_groups = legendre.shape[0]
    lat_count = lax.axis_size("lat")
    northern = lax.axis_index("lat") < lat_count // 2
    count = assign.shape[0]
    chosen = assign[:, None] == lax.iota(jnp.int32, count)[None, :]
    ordered = jnp.einsum(
        "iw,wsfr->isfr", chosen.astype(BF16), fourier, preferred_element_type=F32
    ).astype(BF16)
    gathered = lax.all_to_all(ordered, "ma", split_axis=0, concat_axis=2, tiled=True)
    sym_part, anti_part = fold_pairs(gathered, northern)
    all_ids = jnp.sum(jnp.where(chosen, window[None, :], 0), axis=1)
    group_ids = lax.dynamic_slice_in_dim(
        all_ids, lax.axis_index("ma") * local_groups, local_groups
    )
    column_count = legendre.shape[3]
    wave_total = 2 * column_count
    zero_value = jnp.zeros((), BF16)

    def half_term(parity):
        column = 2 * lax.iota(jnp.int32, column_count) + parity
        upper_slot = (column[None, :] >= wave_total - group_ids[:, None])[:, None, :]
        table_part = legendre[:, :, parity, :]
        masked = jnp.stack(
            [
                jnp.where(upper_slot, zero_value, table_part),
                jnp.where(upper_slot, table_part, zero_value),
            ],
            axis=1,
        )
        leading = sym_part[:, 0] if parity == 0 else anti_part[:, 0]
        flipped = ((group_ids + parity) % 2 == 1)[:, None, None]
        trailing = jnp.where(flipped, anti_part[:, 1], sym_part[:, 1])
        sources = jnp.stack([leading, trailing], axis=1)
        return jnp.einsum("gspk,gsfp->gkf", masked, sources, preferred_element_type=F32)

    partials = jnp.stack([half_term(0), half_term(1)], axis=1)
    return lax.psum_scatter(
        partials.astype(BF16), "lat", scatter_dimension=2, tiled=True
    ).astype(F32)


def fused_kernel(
    lat_n,
    ma_n,
    assign_hbm,
    window_hbm,
    four_hbm,
    leg_hbm,
    sums_ref,
    out_ref,
    assign_ref,
    window_ref,
    four_ref,
    leg_ref,
    stage,
    recv,
    weight,
    part,
    relay,
    landed,
    total,
    send_sem,
    recv_sem,
    psend_sem,
    precv_sem,
    own_sem,
    sum_sem,
    load_sem,
    here_sem,
    late_sem,
):
    groups_here = leg_ref.shape[0]
    fields_here = four_ref.shape[2]
    rows = four_ref.shape[3]
    pair = rows // 2
    body = pair // 128 * 128
    tail = pair - body
    kcols = leg_ref.shape[3]
    block = kcols // lat_n
    hemi = lat_n // 2
    half_ma = ma_n // 2
    half_f = half_ma * fields_here

    lat = lax.axis_index("lat")
    ma = lax.axis_index("ma")
    side = lat // hemi
    mine = side
    partner = lax.rem(lat + hemi, lat_n)
    my_half = ma // half_ma

    beside = lat + 1 - 2 * lax.rem(lat, 2)
    across = lax.rem(beside + hemi, lat_n)

    assign_copy = pltpu.make_async_copy(assign_hbm, assign_ref, load_sem.at[0])
    window_copy = pltpu.make_async_copy(window_hbm, window_ref, load_sem.at[1])
    rows_copy = pltpu.make_async_copy(four_hbm, four_ref, load_sem.at[2])
    table_copy = pltpu.make_async_copy(leg_hbm, leg_ref, load_sem.at[3])
    assign_copy.start()
    rows_copy.start()

    far_first = (1 - my_half) * half_ma
    near_first = my_half * half_ma
    low = lax.rem(ma, 2)

    chip = lax.rem(ma // 2, 2)
    facing = far_first + 2 * (1 - chip)
    other = far_first + 2 * chip
    far = facing + low

    def signal(semaphore, there, q):
        pl.semaphore_signal(semaphore, inc=1, device_id=(there, q), device_id_type=MESH)

    def signal_chip(semaphore, first):
        for m in range(2):
            for there in (lat, partner):
                signal(semaphore, there, first + m)

    def signal_rest(semaphore):
        signal_chip(semaphore, other)
        for there in (beside, across):
            signal(semaphore, there, far)

    barrier = pltpu.get_barrier_semaphore()
    signal_chip(barrier, facing)

    @pl.when(my_half == 0)
    def _():
        signal_rest(barrier)

    window_copy.start()
    table_copy.start()

    def pack(q, g):
        slab = four_ref.at[assign_ref[q * groups_here + g]]
        for t in range(2):
            at, rest = t * (pair + tail), body + t * tail
            stage[g, q, t] = jnp.concatenate(
                [slab[n, :, at : at + body] for n in range(2)]
                + [slab[n, :, rest : rest + tail] for n in range(2)],
                axis=1,
            )

    def row_copy(g, q, own):
        t = mine if own else 1 - mine
        return pltpu.make_async_remote_copy(
            src_ref=stage.at[g, q, t],
            dst_ref=recv.at[g, side, ma],
            send_sem=send_sem.at[g, q, t],
            recv_sem=recv_sem.at[g, side, ma],
            device_id=(lat if own else partner, q),
            device_id_type=MESH,
        )

    def place(hop, turn=0, core=low):
        return lax.rem(hop // 2 + turn, 2) * 2 + lax.rem(hop + core, 2)

    def send_far(hop, g):
        if g == 0:
            q = far_first + place(hop, (1 - chip) * (1 - my_half))
        else:
            q = far_first + place(hop, 0, 0)
        pack(q, g)
        row_copy(g, q, False).start()
        row_copy(g, q, True).start()

    def send_near(hop, g):
        q = near_first + place(hop)
        pack(q, g)
        row_copy(g, q, False).start()

        @pl.when(q != ma)
        def _():
            row_copy(g, q, True).start()

        @pl.when(q == ma)
        def _():
            pltpu.make_async_copy(
                stage.at[g, q, mine], recv.at[g, side, ma], recv_sem.at[g, side, ma]
            ).start()

    def each_hop(step, first=0, end=half_ma):
        def body_of(hop, c):
            step(hop)
            return c

        lax.fori_loop(first, end, body_of, 0)

    pl.semaphore_wait(barrier, 4 + 6 * my_half)

    @pl.when(my_half == 1)
    def _():
        signal_rest(late_sem)
        signal(here_sem, lat, far)

    assign_copy.wait()
    rows_copy.wait()
    each_hop(lambda hop: send_far(hop, 0), 0, half_ma // 2)

    @pl.when(my_half == 0)
    def _():
        pl.semaphore_wait(late_sem, 6)
        signal(here_sem, lat, far)

    pl.semaphore_wait(here_sem, 1)
    each_hop(lambda hop: send_near(hop, 0))
    each_hop(lambda hop: send_far(hop, 0), half_ma // 2)
    each_hop(lambda hop: send_near(hop, 1))
    each_hop(lambda hop: send_far(hop, 1))
    window_copy.wait()
    table_copy.wait()

    ids = [window_ref[assign_ref[ma * groups_here + g]] for g in range(groups_here)]
    for g in range(groups_here):
        for e in range(2):

            def fill(j, c, g=g, e=e):
                start = pl.multiple_of(j * 128, 128)
                table = jnp.concatenate(
                    [
                        leg_ref[g, pl.ds(mine * tail, body), e, pl.ds(start, 128)],
                        leg_ref[g, pl.ds((1 - mine) * body, tail), e, pl.ds(start, 128)],
                    ],
                    axis=0,
                ).astype(F32).T
                k = start + lax.broadcasted_iota(jnp.int32, (128, 1), 0)
                under = 2 * k + e < 2 * kcols - ids[g]
                lower = jnp.where(under, table, 0.0)
                upper = jnp.where(under, 0.0, table)
                weight[g, e, pl.ds(start, 128), :] = jnp.concatenate(
                    [lower[:, :body], upper[:, :body], lower[:, body:], upper[:, body:]],
                    axis=1,
                ).astype(BF16)
                return c

            lax.fori_loop(0, kcols // 128, fill, 0)

    lane = lax.broadcasted_iota(jnp.int32, (1, rows), 1)
    in_upper = ((lane >= body) & (lane < 2 * body)) | (lane >= 2 * body + tail)

    chunks = [(g, j) for j in range(2) for g in range(groups_here)]
    last = len(chunks) - 1

    def remote(c, e, k, source, target, there):
        return pltpu.make_async_remote_copy(
            src_ref=source,
            dst_ref=target,
            send_sem=psend_sem.at[c, e, k],
            recv_sem=precv_sem.at[c, e, k],
            device_id=(there, ma),
            device_id_type=MESH,
        )

    half_block = block // 2

    def piece_of(ref, c, k):
        if c < last or k == 0:
            return ref.at[k]
        return ref.at[1, pl.ds((k - 1) * half_block, half_block)]

    def own_copy(k):
        return pltpu.make_async_copy(
            piece_of(part.at[last, lat], last, k),
            piece_of(out_ref.at[0], last, k),
            own_sem.at[k],
        )

    def beside_copy(c, k):
        target = out_ref.at[1] if c == last else landed.at[0, c]
        source = piece_of(part.at[c, beside], c, k)
        return remote(c, k, 0, source, piece_of(target, c, k), beside)

    def across_copy(c, k):
        source = piece_of(part.at[c, across], c, k)
        if c == last:
            return remote(c, k, 1, source, piece_of(out_ref.at[3], c, k), across)
        return remote(c, k, 1, source, relay.at[c, k], beside)

    def partner_copy(c, k):
        target = out_ref.at[2] if c == last else landed.at[1, c]
        source = piece_of(part.at[c, partner], c, k)
        return remote(c, k, 2, source, piece_of(target, c, k), partner)

    def sum_copy(c):
        return pltpu.make_async_copy(total.at[c], sums_ref.at[c], sum_sem.at[c])

    def arrive(g, m):
        for ns in range(2):
            piece = recv.at[g, ns, m]
            pltpu.make_async_copy(piece, piece, recv_sem.at[g, ns, m]).wait()

    def source_of(g, e, north, south):
        odd = lax.rem(ids[g] + e, 2).astype(F32)
        sign = jnp.where(in_upper, 1.0 - 2.0 * odd, 1.0 - 2.0 * e)
        return (north + sign * south).astype(BF16)

    def product(g, e, d, source):
        return lax.dot_general(
            weight[g, e, pl.ds(pl.multiple_of(d * block, 16), block), :],
            source,
            (((1,), (1,)), ((), ())),
            preferred_element_type=F32,
        )

    def send_parts(c, k, value):
        for d in (across, beside, partner, lat):
            if c < last or k == 0:
                part[c, d, k] = value(d).astype(BF16)
            else:
                part[c, d, 1, pl.ds((k - 1) * half_block, half_block)] = value(d).astype(BF16)
            if d is across:
                across_copy(c, k).start()
            elif d is beside:
                beside_copy(c, k).start()
            elif c == last and d is partner:
                partner_copy(c, k).start()
            elif c == last:
                own_copy(k).start()

    def multiply(c):
        g, j = chunks[c]
        first = lax.rem(my_half + j, 2) * half_ma

        def each(m, v):
            arrive(g, first + m)
            return v

        lax.fori_loop(0, half_ma, each, 0)
        north = recv[g, 0, pl.ds(first, half_ma)].reshape(half_f, rows).astype(F32)
        south = recv[g, 1, pl.ds(first, half_ma)].reshape(half_f, rows).astype(F32)
        for e in range(2):
            source = source_of(g, e, north, south)
            send_parts(c, e, lambda d, e=e, source=source: product(g, e, d, source))

    lanes = lax.broadcasted_iota(jnp.int32, (1, half_f), 1)
    left = lanes < half_f // 2
    even_lane = lax.rem(lanes, half_f // 2) < half_f // 4

    def multiply_outer():
        g = chunks[last][0]
        chips = half_ma // 2
        first = far_first + chips * (1 - my_half)
        for m in range(chips):
            arrive(g, first + m)
        north, south = (
            recv[g, ns, pl.ds(first, chips)].reshape(half_f // 2, rows).astype(F32)
            for ns in range(2)
        )
        source = jnp.concatenate([source_of(g, e, north, south) for e in range(2)], axis=0)
        send_parts(
            last,
            0,
            lambda d: jnp.where(left, product(g, 0, d, source), product(g, 1, d, source)),
        )

    def multiply_inner(k):
        g = chunks[last][0]
        m = far_first + half_ma // 2 * my_half + 2 - k
        arrive(g, m)
        north, south = (recv[g, ns, m].astype(F32) for ns in range(2))
        source = jnp.concatenate([source_of(g, e, north, south) for e in range(2)] * 2, axis=0)

        def value(d):
            both = jnp.where(even_lane, product(g, 0, d, source), product(g, 1, d, source))
            return jnp.where(left, both[:half_block], both[half_block:])

        send_parts(last, k, value)

    def pass_on(c):
        for e in range(2):
            across_copy(c, e).wait_recv()
            total = part[c, partner, e].astype(F32) + relay[c, e].astype(F32)
            part[c, partner, e] = total.astype(BF16)
            partner_copy(c, e).start()

    def finish(c):
        for e in range(2):
            beside_copy(c, e).wait_recv()
            partner_copy(c, e).wait_recv()
            total[c, e] = (
                part[c, lat, e].astype(F32)
                + landed[0, c, e].astype(F32)
                + landed[1, c, e].astype(F32)
            )
        sum_copy(c).start()

    multiply(0)
    multiply(2)
    pass_on(0)
    multiply(1)
    pass_on(2)
    multiply_outer()
    finish(0)
    pass_on(1)
    finish(2)
    multiply_inner(1)
    multiply_inner(2)
    finish(1)
    for g in range(groups_here):

        def sent(q, c, g=g):
            row_copy(g, q, False).wait_send()

            @pl.when(q != ma)
            def _():
                row_copy(g, q, True).wait_send()

            return c

        lax.fori_loop(0, ma_n, sent, 0)
    for c in range(last):
        for e in range(2):
            beside_copy(c, e).wait_send()
            across_copy(c, e).wait_send()
            partner_copy(c, e).wait_send()
        sum_copy(c).wait()
    for k in range(3):
        own_copy(k).wait()
        beside_copy(last, k).wait()
        across_copy(last, k).wait()
        partner_copy(last, k).wait()


def sum_kernel(ma_n, sums_ref, held, out_hbm, total, out_sem):
    last = sums_ref.shape[0]
    groups_here = (last + 1) // 2
    half_f = held.shape[3]
    my_half = lax.axis_index("ma") // (ma_n // 2)

    def store(c):
        at = pl.multiple_of(lax.rem(my_half + c // groups_here, 2) * half_f, 128)
        return pltpu.make_async_copy(
            total if c == last else sums_ref.at[c],
            out_hbm.at[c % groups_here, :, :, pl.ds(at, half_f)],
            out_sem.at[c],
        )

    for c in range(last):
        store(c).start()
    first, second = (
        held[0, k].astype(F32)
        + held[1, k].astype(F32)
        + held[2, k].astype(F32)
        + held[3, k].astype(F32)
        for k in range(2)
    )
    rows = second.shape[0] // 2
    core1, core0 = second[:rows], second[rows:]
    width = half_f // 4
    for e in range(2):
        inner = jnp.concatenate(
            [
                jnp.concatenate([core0[:, at : at + width], core1[:, at : at + width]], axis=1)
                for at in (e * width, (2 + e) * width)
            ],
            axis=0,
        )
        outer = first[:, 2 * e * width : 2 * (e + 1) * width]
        total[e] = jnp.concatenate(
            [jnp.where(my_half == 0, inner, outer), jnp.where(my_half == 0, outer, inner)],
            axis=1,
        )
    store(last).start()
    for c in range(last + 1):
        store(c).wait()


def fused_on_device(fourier, legendre, window, assign):
    lat_n, ma_n = lax.axis_size("lat"), lax.axis_size("ma")
    _, slots, fields_here, rows = fourier.shape
    groups_here, pair, parities, kcols = legendre.shape
    block = kcols // lat_n
    fields = fields_here * ma_n
    chunks = 2 * groups_here
    half_f = fields // 2
    hbm = pl.BlockSpec(memory_space=pltpu.HBM)
    anywhere = pl.BlockSpec(memory_space=pl.ANY)
    dma = pltpu.SemaphoreType.DMA
    sums, parts = pl.pallas_call(
        functools.partial(fused_kernel, lat_n, ma_n),
        out_shape=(
            jax.ShapeDtypeStruct((chunks - 1, 2, block, half_f), F32),
            jax.ShapeDtypeStruct((4, 2, block, half_f), BF16),
        ),
        in_specs=[hbm, hbm, hbm, hbm],
        out_specs=(anywhere, anywhere),
        scratch_shapes=[
            pltpu.SMEM(assign.shape, jnp.int32),
            pltpu.SMEM(window.shape, jnp.int32),
            pltpu.VMEM(fourier.shape, BF16),
            pltpu.VMEM(legendre.shape, BF16),
            pltpu.VMEM((groups_here, ma_n, 2, fields_here, rows), BF16),
            pltpu.VMEM((groups_here, 2, ma_n, fields_here, rows), BF16),
            pltpu.VMEM((groups_here, 2, kcols, rows), BF16),
            pltpu.VMEM((chunks, lat_n, 2, block, half_f), BF16),
            pltpu.VMEM((chunks - 1, 2, block, half_f), BF16),
            pltpu.VMEM((2, chunks - 1, 2, block, half_f), BF16),
            pltpu.VMEM((chunks - 1, 2, block, half_f), F32),
            dma((groups_here, ma_n, 2)),
            dma((groups_here, 2, ma_n)),
            dma((chunks, 3, 3)),
            dma((chunks, 3, 3)),
            dma((3,)),
            dma((chunks - 1,)),
            dma((4,)),
            pltpu.SemaphoreType.REGULAR,
            pltpu.SemaphoreType.REGULAR,
        ],
        compiler_params=pltpu.CompilerParams(
            collective_id=0, has_side_effects=True, vmem_limit_bytes=24 * 2**20
        ),
        cost_estimate=pl.CostEstimate(
            flops=8 * groups_here * kcols * rows * fields,
            bytes_accessed=2 * (fourier.size + legendre.size),
            transcendentals=0,
        ),
    )(*(pltpu.with_memory_space_constraint(x, pltpu.HBM) for x in (assign, window, fourier, legendre)))
    return pl.pallas_call(
        functools.partial(sum_kernel, ma_n),
        out_shape=jax.ShapeDtypeStruct((groups_here, 2, block, fields), F32),
        in_specs=[anywhere, pl.BlockSpec(memory_space=pltpu.VMEM)],
        out_specs=hbm,
        scratch_shapes=[
            pltpu.VMEM((2, block, half_f), F32),
            dma((chunks,)),
        ],
        compiler_params=pltpu.CompilerParams(vmem_limit_bytes=16 * 2**20),
        cost_estimate=pl.CostEstimate(
            flops=parts.size, bytes_accessed=4 * parts.size, transcendentals=0
        ),
    )(sums, parts)


def fits_kernel(mesh, fourier, legendre):
    lat_n, ma_n = mesh.shape["lat"], mesh.shape["ma"]
    fields_here = fourier.shape[2] // ma_n
    pair = legendre.shape[1] // lat_n
    block = legendre.shape[3] // lat_n
    return (
        fourier.shape[1] == 2
        and lat_n == 4
        and ma_n == 8
        and legendre.shape[0] == 2 * ma_n
        and fields_here % 16 == 0
        and (fields_here * ma_n) % 256 == 0
        and (2 * pair) % 128 == 0
        and block % 32 == 0
        and legendre.shape[3] % 128 == 0
    )


def solution(mesh):
    def run(fourier, legendre, window, assign):
        fused = fits_kernel(mesh, fourier, legendre)
        return jax.shard_map(
            fused_on_device if fused else plain_on_device,
            mesh=mesh,
            in_specs=(P(None, None, "ma", "lat"), P("ma", "lat", None, None), P(), P()),
            out_specs=P("ma", None, "lat", None),
            check_vma=False,
        )(fourier, legendre, window, assign)

    return run
```

```python
import functools

import jax
import jax.numpy as jnp
from jax import lax
from jax.experimental import pallas as pl
from jax.experimental.pallas import tpu as pltpu
from jax.sharding import PartitionSpec as P

MESH = pl.DeviceIdType.MESH
BF16 = jnp.bfloat16
F32 = jnp.float32


def swapped(value, axis, bit):
    mask = 2**bit
    pairs = [(source, source ^ mask) for source in range(lax.axis_size(axis))]
    return lax.ppermute(value, axis, pairs)


def fold_pairs(latitudes, northern):
    pair_rows = latitudes.shape[3] // 2
    leading_rows = latitudes[:, :, :, :pair_rows]
    trailing_rows = latitudes[:, :, :, pair_rows:]
    outgoing = jnp.where(northern, trailing_rows, leading_rows)
    bit_number = lax.axis_size("lat").bit_length() - 2
    arrived = swapped(outgoing, "lat", bit_number)
    staying = jnp.where(northern, leading_rows, trailing_rows)
    upper_rows = jnp.where(northern, staying, arrived).astype(F32)
    lower_rows = jnp.where(northern, arrived, staying).astype(F32)
    return (
        (upper_rows + lower_rows).astype(BF16),
        (upper_rows - lower_rows).astype(BF16),
    )


def plain_on_device(fourier, legendre, window, assign):
    local_groups = legendre.shape[0]
    lat_count = lax.axis_size("lat")
    northern = lax.axis_index("lat") < lat_count // 2
    count = assign.shape[0]
    chosen = assign[:, None] == lax.iota(jnp.int32, count)[None, :]
    ordered = jnp.einsum(
        "iw,wsfr->isfr", chosen.astype(BF16), fourier, preferred_element_type=F32
    ).astype(BF16)
    gathered = lax.all_to_all(ordered, "ma", split_axis=0, concat_axis=2, tiled=True)
    sym_part, anti_part = fold_pairs(gathered, northern)
    all_ids = jnp.sum(jnp.where(chosen, window[None, :], 0), axis=1)
    group_ids = lax.dynamic_slice_in_dim(
        all_ids, lax.axis_index("ma") * local_groups, local_groups
    )
    column_count = legendre.shape[3]
    wave_total = 2 * column_count
    zero_value = jnp.zeros((), BF16)

    def half_term(parity):
        column = 2 * lax.iota(jnp.int32, column_count) + parity
        upper_slot = (column[None, :] >= wave_total - group_ids[:, None])[:, None, :]
        table_part = legendre[:, :, parity, :]
        masked = jnp.stack(
            [
                jnp.where(upper_slot, zero_value, table_part),
                jnp.where(upper_slot, table_part, zero_value),
            ],
            axis=1,
        )
        leading = sym_part[:, 0] if parity == 0 else anti_part[:, 0]
        flipped = ((group_ids + parity) % 2 == 1)[:, None, None]
        trailing = jnp.where(flipped, anti_part[:, 1], sym_part[:, 1])
        sources = jnp.stack([leading, trailing], axis=1)
        return jnp.einsum("gspk,gsfp->gkf", masked, sources, preferred_element_type=F32)

    partials = jnp.stack([half_term(0), half_term(1)], axis=1)
    return lax.psum_scatter(
        partials.astype(BF16), "lat", scatter_dimension=2, tiled=True
    ).astype(F32)


def fused_kernel(
    lat_n,
    ma_n,
    assign_hbm,
    window_hbm,
    four_hbm,
    leg_hbm,
    sums_ref,
    out_ref,
    assign_ref,
    window_ref,
    four_ref,
    leg_ref,
    stage,
    recv,
    weight,
    part,
    relay,
    landed,
    total,
    send_sem,
    recv_sem,
    psend_sem,
    precv_sem,
    own_sem,
    sum_sem,
    load_sem,
    here_sem,
    late_sem,
):
    groups_here = leg_ref.shape[0]
    fields_here = four_ref.shape[2]
    rows = four_ref.shape[3]
    pair = rows // 2
    body = pair // 128 * 128
    tail = pair - body
    kcols = leg_ref.shape[3]
    block = kcols // lat_n
    hemi = lat_n // 2
    half_ma = ma_n // 2
    half_f = half_ma * fields_here

    lat = lax.axis_index("lat")
    ma = lax.axis_index("ma")
    side = lat // hemi
    mine = side
    partner = lax.rem(lat + hemi, lat_n)
    my_half = ma // half_ma

    beside = lat + 1 - 2 * lax.rem(lat, 2)
    across = lax.rem(beside + hemi, lat_n)

    assign_copy = pltpu.make_async_copy(assign_hbm, assign_ref, load_sem.at[0])
    window_copy = pltpu.make_async_copy(window_hbm, window_ref, load_sem.at[1])
    rows_copy = pltpu.make_async_copy(four_hbm, four_ref, load_sem.at[2])
    table_copy = pltpu.make_async_copy(leg_hbm, leg_ref, load_sem.at[3])
    assign_copy.start()
    rows_copy.start()

    far_first = (1 - my_half) * half_ma
    near_first = my_half * half_ma
    low = lax.rem(ma, 2)

    chip = lax.rem(ma // 2, 2)
    facing = far_first + 2 * (1 - chip)
    other = far_first + 2 * chip
    far = facing + low

    def signal(semaphore, there, q):
        pl.semaphore_signal(semaphore, inc=1, device_id=(there, q), device_id_type=MESH)

    def signal_chip(semaphore, first):
        for m in range(2):
            for there in (lat, partner):
                signal(semaphore, there, first + m)

    barrier = pltpu.get_barrier_semaphore()
    signal_chip(barrier, facing)

    @pl.when(my_half == 0)
    def _():
        signal_chip(barrier, other)
        for there in (beside, across):
            signal(barrier, there, ma)

    window_copy.start()
    table_copy.start()

    def pack(q, g):
        slab = four_ref.at[assign_ref[q * groups_here + g]]
        for t in range(2):
            at, rest = t * (pair + tail), body + t * tail
            stage[g, q, t] = jnp.concatenate(
                [slab[n, :, at : at + body] for n in range(2)]
                + [slab[n, :, rest : rest + tail] for n in range(2)],
                axis=1,
            )

    def row_copy(g, q, own):
        t = mine if own else 1 - mine
        return pltpu.make_async_remote_copy(
            src_ref=stage.at[g, q, t],
            dst_ref=recv.at[g, side, ma],
            send_sem=send_sem.at[g, q, t],
            recv_sem=recv_sem.at[g, side, ma],
            device_id=(lat if own else partner, q),
            device_id_type=MESH,
        )

    def place(hop, turn=0, core=low):
        return lax.rem(hop // 2 + turn, 2) * 2 + lax.rem(hop + core, 2)

    def send_far(hop, g):
        if g == 0:
            q = far_first + place(hop, (1 - chip) * (1 - my_half))
        else:
            q = far_first + place(hop, 0, 0)
        pack(q, g)
        row_copy(g, q, False).start()
        row_copy(g, q, True).start()

    def send_near(hop, g):
        q = near_first + place(hop)
        pack(q, g)
        row_copy(g, q, False).start()

        @pl.when(q != ma)
        def _():
            row_copy(g, q, True).start()

        @pl.when(q == ma)
        def _():
            pltpu.make_async_copy(
                stage.at[g, q, mine], recv.at[g, side, ma], recv_sem.at[g, side, ma]
            ).start()

    def each_hop(step, first=0, end=half_ma):
        def body_of(hop, c):
            step(hop)
            return c

        lax.fori_loop(first, end, body_of, 0)

    pl.semaphore_wait(barrier, 6 + 2 * my_half)

    @pl.when(my_half == 1)
    def _():
        signal_chip(late_sem, other)
        signal(here_sem, lat, far)

    @pl.when(my_half == 0)
    def _():
        signal(late_sem, beside, ma)

    assign_copy.wait()
    rows_copy.wait()
    each_hop(lambda hop: send_far(hop, 0), 0, half_ma // 2)

    @pl.when(my_half == 0)
    def _():
        pl.semaphore_wait(late_sem, 5)
        signal(here_sem, lat, far)

    pl.semaphore_wait(here_sem, 1)
    each_hop(lambda hop: send_near(hop, 0))
    each_hop(lambda hop: send_far(hop, 0), half_ma // 2)
    each_hop(lambda hop: send_near(hop, 1))
    each_hop(lambda hop: send_far(hop, 1))
    window_copy.wait()
    table_copy.wait()

    ids = [window_ref[assign_ref[ma * groups_here + g]] for g in range(groups_here)]
    for g in range(groups_here):
        for e in range(2):

            def fill(j, c, g=g, e=e):
                start = pl.multiple_of(j * 128, 128)
                table = jnp.concatenate(
                    [
                        leg_ref[g, pl.ds(mine * tail, body), e, pl.ds(start, 128)],
                        leg_ref[g, pl.ds((1 - mine) * body, tail), e, pl.ds(start, 128)],
                    ],
                    axis=0,
                ).astype(F32).T
                k = start + lax.broadcasted_iota(jnp.int32, (128, 1), 0)
                under = 2 * k + e < 2 * kcols - ids[g]
                lower = jnp.where(under, table, 0.0)
                upper = jnp.where(under, 0.0, table)
                weight[g, e, pl.ds(start, 128), :] = jnp.concatenate(
                    [lower[:, :body], upper[:, :body], lower[:, body:], upper[:, body:]],
                    axis=1,
                ).astype(BF16)
                return c

            lax.fori_loop(0, kcols // 128, fill, 0)

    lane = lax.broadcasted_iota(jnp.int32, (1, rows), 1)
    in_upper = ((lane >= body) & (lane < 2 * body)) | (lane >= 2 * body + tail)

    chunks = [(g, j) for j in range(2) for g in range(groups_here)]
    last = len(chunks) - 1

    def remote(c, e, k, source, target, there):
        return pltpu.make_async_remote_copy(
            src_ref=source,
            dst_ref=target,
            send_sem=psend_sem.at[c, e, k],
            recv_sem=precv_sem.at[c, e, k],
            device_id=(there, ma),
            device_id_type=MESH,
        )

    half_block = block // 2

    def piece_of(ref, c, k):
        if c < last or k == 0:
            return ref.at[k]
        return ref.at[1, pl.ds((k - 1) * half_block, half_block)]

    def own_copy(k):
        return pltpu.make_async_copy(
            piece_of(part.at[last, lat], last, k),
            piece_of(out_ref.at[0], last, k),
            own_sem.at[k],
        )

    def beside_copy(c, k):
        target = out_ref.at[1] if c == last else landed.at[0, c]
        source = piece_of(part.at[c, beside], c, k)
        return remote(c, k, 0, source, piece_of(target, c, k), beside)

    def across_copy(c, k):
        source = piece_of(part.at[c, across], c, k)
        if c == last:
            return remote(c, k, 1, source, piece_of(out_ref.at[3], c, k), across)
        return remote(c, k, 1, source, relay.at[c, k], beside)

    def partner_copy(c, k):
        target = out_ref.at[2] if c == last else landed.at[1, c]
        source = piece_of(part.at[c, partner], c, k)
        return remote(c, k, 2, source, piece_of(target, c, k), partner)

    def sum_copy(c):
        return pltpu.make_async_copy(total.at[c], sums_ref.at[c], sum_sem.at[c])

    def arrive(g, m):
        for ns in range(2):
            piece = recv.at[g, ns, m]
            pltpu.make_async_copy(piece, piece, recv_sem.at[g, ns, m]).wait()

    def source_of(g, e, north, south):
        odd = lax.rem(ids[g] + e, 2).astype(F32)
        sign = jnp.where(in_upper, 1.0 - 2.0 * odd, 1.0 - 2.0 * e)
        return (north + sign * south).astype(BF16)

    def product(g, e, d, source):
        return lax.dot_general(
            weight[g, e, pl.ds(pl.multiple_of(d * block, 16), block), :],
            source,
            (((1,), (1,)), ((), ())),
            preferred_element_type=F32,
        )

    def send_parts(c, k, value):
        for d in (across, beside, partner, lat):
            if c < last or k == 0:
                part[c, d, k] = value(d).astype(BF16)
            else:
                part[c, d, 1, pl.ds((k - 1) * half_block, half_block)] = value(d).astype(BF16)
            if d is across:
                across_copy(c, k).start()
            elif d is beside:
                beside_copy(c, k).start()
            elif c == last and d is partner:
                partner_copy(c, k).start()
            elif c == last:
                own_copy(k).start()

    def multiply(c):
        g, j = chunks[c]
        first = lax.rem(my_half + j, 2) * half_ma

        def each(m, v):
            arrive(g, first + m)
            return v

        lax.fori_loop(0, half_ma, each, 0)
        north = recv[g, 0, pl.ds(first, half_ma)].reshape(half_f, rows).astype(F32)
        south = recv[g, 1, pl.ds(first, half_ma)].reshape(half_f, rows).astype(F32)
        for e in range(2):
            source = source_of(g, e, north, south)
            send_parts(c, e, lambda d, e=e, source=source: product(g, e, d, source))

    lanes = lax.broadcasted_iota(jnp.int32, (1, half_f), 1)
    left = lanes < half_f // 2
    even_lane = lax.rem(lanes, half_f // 2) < half_f // 4

    def multiply_outer():
        g = chunks[last][0]
        chips = half_ma // 2
        first = far_first + chips * (1 - my_half)
        for m in range(chips):
            arrive(g, first + m)
        north, south = (
            recv[g, ns, pl.ds(first, chips)].reshape(half_f // 2, rows).astype(F32)
            for ns in range(2)
        )
        source = jnp.concatenate([source_of(g, e, north, south) for e in range(2)], axis=0)
        send_parts(
            last,
            0,
            lambda d: jnp.where(left, product(g, 0, d, source), product(g, 1, d, source)),
        )

    def multiply_inner(k):
        g = chunks[last][0]
        m = far_first + half_ma // 2 * my_half + 2 - k
        arrive(g, m)
        north, south = (recv[g, ns, m].astype(F32) for ns in range(2))
        source = jnp.concatenate([source_of(g, e, north, south) for e in range(2)] * 2, axis=0)

        def value(d):
            both = jnp.where(even_lane, product(g, 0, d, source), product(g, 1, d, source))
            return jnp.where(left, both[:half_block], both[half_block:])

        send_parts(last, k, value)

    def pass_on(c):
        for e in range(2):
            across_copy(c, e).wait_recv()
            total = part[c, partner, e].astype(F32) + relay[c, e].astype(F32)
            part[c, partner, e] = total.astype(BF16)
            partner_copy(c, e).start()

    def finish(c):
        for e in range(2):
            beside_copy(c, e).wait_recv()
            partner_copy(c, e).wait_recv()
            total[c, e] = (
                part[c, lat, e].astype(F32)
                + landed[0, c, e].astype(F32)
                + landed[1, c, e].astype(F32)
            )
        sum_copy(c).start()

    multiply(0)
    multiply(2)
    pass_on(0)
    multiply(1)
    pass_on(2)

    @pl.when(chip == 1)
    def _():
        pass_on(1)

    multiply_outer()
    finish(0)

    @pl.when(chip == 0)
    def _():
        pass_on(1)

    finish(2)
    multiply_inner(1)
    multiply_inner(2)
    finish(1)
    for g in range(groups_here):

        def sent(q, c, g=g):
            row_copy(g, q, False).wait_send()

            @pl.when(q != ma)
            def _():
                row_copy(g, q, True).wait_send()

            return c

        lax.fori_loop(0, ma_n, sent, 0)
    for c in range(last):
        for e in range(2):
            beside_copy(c, e).wait_send()
            across_copy(c, e).wait_send()
            partner_copy(c, e).wait_send()
        sum_copy(c).wait()
    for k in range(3):
        own_copy(k).wait()
        beside_copy(last, k).wait()
        across_copy(last, k).wait()
        partner_copy(last, k).wait()


def sum_kernel(ma_n, sums_ref, held, out_hbm, total, out_sem):
    last = sums_ref.shape[0]
    groups_here = (last + 1) // 2
    half_f = held.shape[3]
    my_half = lax.axis_index("ma") // (ma_n // 2)

    def store(c):
        at = pl.multiple_of(lax.rem(my_half + c // groups_here, 2) * half_f, 128)
        return pltpu.make_async_copy(
            total if c == last else sums_ref.at[c],
            out_hbm.at[c % groups_here, :, :, pl.ds(at, half_f)],
            out_sem.at[c],
        )

    for c in range(last):
        store(c).start()
    first, second = (
        held[0, k].astype(F32)
        + held[1, k].astype(F32)
        + held[2, k].astype(F32)
        + held[3, k].astype(F32)
        for k in range(2)
    )
    rows = second.shape[0] // 2
    core1, core0 = second[:rows], second[rows:]
    width = half_f // 4
    for e in range(2):
        inner = jnp.concatenate(
            [
                jnp.concatenate([core0[:, at : at + width], core1[:, at : at + width]], axis=1)
                for at in (e * width, (2 + e) * width)
            ],
            axis=0,
        )
        outer = first[:, 2 * e * width : 2 * (e + 1) * width]
        total[e] = jnp.concatenate(
            [jnp.where(my_half == 0, inner, outer), jnp.where(my_half == 0, outer, inner)],
            axis=1,
        )
    store(last).start()
    for c in range(last + 1):
        store(c).wait()


def fused_on_device(fourier, legendre, window, assign):
    lat_n, ma_n = lax.axis_size("lat"), lax.axis_size("ma")
    _, slots, fields_here, rows = fourier.shape
    groups_here, pair, parities, kcols = legendre.shape
    block = kcols // lat_n
    fields = fields_here * ma_n
    chunks = 2 * groups_here
    half_f = fields // 2
    hbm = pl.BlockSpec(memory_space=pltpu.HBM)
    anywhere = pl.BlockSpec(memory_space=pl.ANY)
    dma = pltpu.SemaphoreType.DMA
    sums, parts = pl.pallas_call(
        functools.partial(fused_kernel, lat_n, ma_n),
        out_shape=(
            jax.ShapeDtypeStruct((chunks - 1, 2, block, half_f), F32),
            jax.ShapeDtypeStruct((4, 2, block, half_f), BF16),
        ),
        in_specs=[hbm, hbm, hbm, hbm],
        out_specs=(anywhere, anywhere),
        scratch_shapes=[
            pltpu.SMEM(assign.shape, jnp.int32),
            pltpu.SMEM(window.shape, jnp.int32),
            pltpu.VMEM(fourier.shape, BF16),
            pltpu.VMEM(legendre.shape, BF16),
            pltpu.VMEM((groups_here, ma_n, 2, fields_here, rows), BF16),
            pltpu.VMEM((groups_here, 2, ma_n, fields_here, rows), BF16),
            pltpu.VMEM((groups_here, 2, kcols, rows), BF16),
            pltpu.VMEM((chunks, lat_n, 2, block, half_f), BF16),
            pltpu.VMEM((chunks - 1, 2, block, half_f), BF16),
            pltpu.VMEM((2, chunks - 1, 2, block, half_f), BF16),
            pltpu.VMEM((chunks - 1, 2, block, half_f), F32),
            dma((groups_here, ma_n, 2)),
            dma((groups_here, 2, ma_n)),
            dma((chunks, 3, 3)),
            dma((chunks, 3, 3)),
            dma((3,)),
            dma((chunks - 1,)),
            dma((4,)),
            pltpu.SemaphoreType.REGULAR,
            pltpu.SemaphoreType.REGULAR,
        ],
        compiler_params=pltpu.CompilerParams(
            collective_id=0, has_side_effects=True, vmem_limit_bytes=24 * 2**20
        ),
        cost_estimate=pl.CostEstimate(
            flops=8 * groups_here * kcols * rows * fields,
            bytes_accessed=2 * (fourier.size + legendre.size),
            transcendentals=0,
        ),
    )(*(pltpu.with_memory_space_constraint(x, pltpu.HBM) for x in (assign, window, fourier, legendre)))
    return pl.pallas_call(
        functools.partial(sum_kernel, ma_n),
        out_shape=jax.ShapeDtypeStruct((groups_here, 2, block, fields), F32),
        in_specs=[anywhere, pl.BlockSpec(memory_space=pltpu.VMEM)],
        out_specs=hbm,
        scratch_shapes=[
            pltpu.VMEM((2, block, half_f), F32),
            dma((chunks,)),
        ],
        compiler_params=pltpu.CompilerParams(vmem_limit_bytes=16 * 2**20),
        cost_estimate=pl.CostEstimate(
            flops=parts.size, bytes_accessed=4 * parts.size, transcendentals=0
        ),
    )(sums, parts)


def fits_kernel(mesh, fourier, legendre):
    lat_n, ma_n = mesh.shape["lat"], mesh.shape["ma"]
    fields_here = fourier.shape[2] // ma_n
    pair = legendre.shape[1] // lat_n
    block = legendre.shape[3] // lat_n
    return (
        fourier.shape[1] == 2
        and lat_n == 4
        and ma_n == 8
        and legendre.shape[0] == 2 * ma_n
        and fields_here % 16 == 0
        and (fields_here * ma_n) % 256 == 0
        and (2 * pair) % 128 == 0
        and block % 32 == 0
        and legendre.shape[3] % 128 == 0
    )


def solution(mesh):
    def run(fourier, legendre, window, assign):
        fused = fits_kernel(mesh, fourier, legendre)
        return jax.shard_map(
            fused_on_device if fused else plain_on_device,
            mesh=mesh,
            in_specs=(P(None, None, "ma", "lat"), P("ma", "lat", None, None), P(), P()),
            out_specs=P("ma", None, "lat", None),
            check_vma=False,
        )(fourier, legendre, window, assign)

    return run
```
